512 devices in a mesh: tile: 128 (over y, z, core), vis: 4 (over x).
Axes of the slice: x: 4, y: 4, z: 16, core: 2. Of those that a mesh axis runs over, the one named last changes fastest.
Arguments:
- model_grid: bfloat16 [4, 65536, 128], P(None, 'tile'), may hold values from -6 to 6
- observed: bfloat16 [4, 8192, 256], P(None, ('tile', 'vis')), may hold values from -6 to 6
- kernels: bfloat16 [8192, 256, 128], P(('tile', 'vis')), may hold values from -0.75 to 0.75
- offsets: int32 [8192, 2], P(('tile', 'vis')), may hold values from 0 to 511, as said below
- counts: int32 [512], P(('tile', 'vis')), may hold values from 8 to 16, as said below
Outputs:
- new_model: bfloat16 [4, 65536, 128], P(None, ('tile', 'vis'))
The draws below stay inside these ranges and needn't reach their ends.
Inputs may be any that keep to these rules, and one draw needn't show every extreme that they name: Column offsets lie in 0 to 64, row offsets in 0 to 511; block 0 sits at row 511 and column 64. `counts`: device 0 has all 16 slots live.
All inputs are finite; a program needn't handle non-finite values.
Results may differ from the reference program's by a relative error of at most 0.0052.
Values may be sent and summed in bfloat16 or wider, within the bound.
No kernel may reach another device: no remote copies, remote signals or barrier semaphores. Data moves between devices by JAX's collectives and lax.ppermute only.
A program may use at most 64 MiB of HBM per device.

```python
import jax
import jax.numpy as jnp
from jax import lax

ROWS = 512
COLS = 128
SUB = 64
K = 256
BLK = 16
ITERS = 2
NU = 65536
BLOCKS = 8192
N_TILE = 128
N_VIS = 4


def draw_offsets(key, part):
    key = jax.random.fold_in(key, 11)
    key_rows, key_cols = jax.random.split(key)
    row_off = jax.random.randint(key_rows, (BLOCKS,), 0, ROWS, dtype=jnp.int32)
    col_off = jax.random.randint(key_cols, (BLOCKS,), 0, COLS - SUB + 1, dtype=jnp.int32)
    row_off = row_off.at[0].set(ROWS - 1).at[1].set(0)
    col_off = col_off.at[0].set(COLS - SUB).at[1].set(0)
    return jnp.stack([row_off, col_off], axis=1).astype(jnp.int32)


def draw_counts(key, part):
    key = jax.random.fold_in(key, 12)
    live = jax.random.randint(key, (N_TILE * N_VIS,), BLK // 2, BLK + 1, dtype=jnp.int32)
    return live.at[0].set(BLK).at[1].set(BLK // 2).astype(jnp.int32)


def steps_of(stream_key, shape, pieces, low, top_value):
    level, own = 1.0, jax.random.fold_in(stream_key, 6)
    for dim, shards_of in pieces:
        steps = jnp.exp(jax.random.uniform(jax.random.fold_in(own, dim), (shards_of,), jnp.float32, low / len(pieces), top_value / len(pieces)))
        level = level * jnp.repeat(steps, shape[dim] // shards_of).reshape([-1 if axis == dim else 1 for axis in range(len(shape))])
    return level


def gaussian(own_key, extent, scale, bound, shards=(), kind=jnp.bfloat16):
    gain = steps_of(own_key, extent, shards, -0.22, 0.18) if shards else 1.0
    drawn = jax.random.normal(own_key, extent, jnp.float32) * scale * gain
    return jnp.minimum(jnp.maximum(drawn, -bound), bound).astype(kind)


def setup_inputs(seed: int = 0) -> dict:
    streams_of = jax.random.split(jax.random.key(seed), 6)
    model_grid = gaussian(streams_of[0], (4, NU, COLS), 1.0, 6.0, ((1, 128),))
    observed = gaussian(streams_of[1], (4, BLOCKS, K), 1.0, 6.0, ((1, 512),))
    kernels = gaussian(streams_of[2], (BLOCKS, K, 2 * SUB), 0.125, 0.75, ((0, 512),))
    offsets = draw_offsets(jax.random.fold_in(streams_of[5], 71), 0)
    counts = draw_counts(jax.random.fold_in(streams_of[5], 71), 0)
    return dict(model_grid=model_grid, observed=observed, kernels=kernels, offsets=offsets, counts=counts)


sign_table = (1.0, -1.0, 1.0, -1.0)
step_size = 0.5


def reference(model_grid, observed, kernels, offsets, counts):
    devices = N_TILE * N_VIS
    parity = jnp.array(sign_table, jnp.float32)[:, None, None]
    block_ids = jnp.arange(devices * BLK, dtype=jnp.int32)
    row_all = offsets[:, 0] + (block_ids // BLK // N_VIS) * ROWS
    row_group = row_all.reshape(devices, BLK)
    col_group = offsets[:, 1].reshape(devices, BLK)
    slot_ids = jnp.arange(BLK, dtype=jnp.int32)
    measured = jnp.transpose(observed, (1, 0, 2)).reshape(devices, BLK, 4, K)
    kern_group = kernels.reshape(devices, BLK, K, 2 * SUB)
    anchor = jnp.zeros((), jnp.int32)
    grid = model_grid
    for cycle in range(ITERS):
        extended = jnp.concatenate([grid, grid[:, :SUB]], axis=1)

        def device_step(accumulated, processor_entry):
            kernel_weights_local, measurement_values, row_offsets_local, column_offsets_local, sample_count_local = processor_entry
            kern_u = kernel_weights_local[:, :, :SUB].astype(jnp.float32)
            kern_v = kernel_weights_local[:, :, SUB:].astype(jnp.float32)

            def cut_block(row_at, col_at):
                return lax.dynamic_slice(extended, (anchor, row_at, col_at), (4, SUB, SUB))

            subgrids = jax.vmap(cut_block)(row_offsets_local, column_offsets_local).astype(jnp.float32)
            inner_sum = jnp.einsum("ncab,nkb->ncak", subgrids, kern_v)
            forward_prediction = jnp.einsum("nka,ncak->nck", kern_u, inner_sum)
            active_slot_index = (slot_ids < sample_count_local)[:, None, None]
            misfit_values = jnp.where(active_slot_index, measurement_values.astype(jnp.float32) - forward_prediction, jnp.float32(0.0))
            weighted = (kern_u[:, None] * misfit_values[..., None]).astype(jnp.bfloat16)
            fresh = jnp.einsum("ncka,nkb->ncab", weighted.astype(jnp.float32), kern_v)

            def place_block(block_id, current_sum):
                start = (anchor, row_offsets_local[block_id], column_offsets_local[block_id])
                current = lax.dynamic_slice(current_sum, start, (4, SUB, SUB))
                return lax.dynamic_update_slice(current_sum, current + fresh[block_id], start)

            return lax.fori_loop(0, BLK, place_block, accumulated), None

        empty = jnp.zeros((4, NU + SUB, COLS), jnp.float32)
        gridded, _ = lax.scan(device_step, empty, (kern_group, measured, row_group, col_group, counts))
        folded = gridded[:, :NU].at[:, :SUB].add(gridded[:, NU:])
        mirrored = folded[:, ::-1, ::-1]
        updated = grid.astype(jnp.float32) + step_size * 0.5 * (folded + parity * mirrored)
        grid = updated.astype(jnp.bfloat16)
    return grid
```

```python
import functools

import jax
import jax.numpy as jnp
from jax import lax
from jax.experimental import pallas as pl
from jax.experimental.pallas import tpu as pltpu
from jax.sharding import PartitionSpec as P

SUB = 64
GROUP = 4
SIGNS = (1.0, -1.0, 1.0, -1.0)
STEP = 0.5 * 0.5
F32 = jnp.float32
BF16 = jnp.bfloat16
VMEM = pl.BlockSpec(memory_space=pltpu.VMEM)
SMEM = pl.BlockSpec(memory_space=pltpu.SMEM)


def send(value, route):
    tiles = lax.axis_size("tile")
    views = lax.axis_size("vis")
    pairs = []
    for tile in range(tiles):
        for view in range(views):
            to_tile, to_view = route(tile, view)
            pairs.append((tile * views + view, to_tile % tiles * views + to_view % views))
    return lax.ppermute(value, ("tile", "vis"), pairs)


def call(body, outs, scratch=(), flops=0, moved=0):
    return functools.partial(
        pl.pallas_call,
        body,
        out_shape=outs,
        scratch_shapes=list(scratch),
        compiler_params=pltpu.CompilerParams(vmem_limit_bytes=40 * 1024 * 1024),
        cost_estimate=pl.CostEstimate(flops=flops, bytes_accessed=moved, transcendentals=0),
    )


def dot_nn(left, right):
    return lax.dot_general(left, right, (((1,), (0,)), ((), ())), preferred_element_type=F32)


def dot_nt(left, right):
    return lax.dot_general(left, right, (((1,), (1,)), ((), ())), preferred_element_type=F32)


def prepare_body(offsets, kern, ku_t, kv_t, kv):
    blocks = kern.shape[0]
    cols = kern.shape[2]

    def one(block):
        shift = SUB - offsets[block, 1]
        row = lax.broadcasted_iota(jnp.int32, (cols, cols), 0)
        col = lax.broadcasted_iota(jnp.int32, (cols, cols), 1)
        place_t = jnp.where((col == row + shift) & (col >= SUB), 1.0, 0.0).astype(BF16)
        place = jnp.where((row == col + shift) & (row >= SUB), 1.0, 0.0).astype(BF16)
        pick = jnp.where(row == col, 1.0, 0.0).astype(BF16)[:SUB]
        weights = kern[block]
        ku_t[block] = dot_nt(pick, weights).astype(BF16)
        kv_t[block] = dot_nt(place_t, weights).astype(BF16)
        kv[block] = dot_nn(weights, place).astype(BF16)

    def group(index, carry):
        for lane in range(GROUP):
            one(index * GROUP + lane)
        return carry

    lax.fori_loop(0, blocks // GROUP, group, 0)


def grid_blocks(picks, limit, offsets, obs, ku_t, kv_t, kv, grid, acc):
    def group(index, carry):
        staged = []
        for lane in range(GROUP):
            place = index * GROUP + lane
            live = place < limit
            block = picks[jnp.minimum(place, limit - 1)]
            row = offsets[block, 0]
            patch = jnp.concatenate(
                [grid[comp, pl.ds(row, SUB), :] for comp in range(4)], axis=0
            ).astype(BF16)
            inner = dot_nn(patch, kv_t[block])
            along_u = ku_t[block].astype(F32)
            parts = []
            for comp in range(4):
                seen = jnp.sum(along_u * inner[comp * SUB : (comp + 1) * SUB], axis=0, keepdims=True)
                left = jnp.where(live, obs[comp, pl.ds(block, 1), :] - seen, 0.0)
                parts.append((along_u * left).astype(BF16))
            fresh = dot_nn(jnp.concatenate(parts, axis=0), kv[block])
            staged.append((row, fresh))
        for row, fresh in staged:
            for comp in range(4):
                acc[comp, pl.ds(row, SUB), :] += fresh[comp * SUB : (comp + 1) * SUB]
        return carry

    lax.fori_loop(0, (limit + GROUP - 1) // GROUP, group, 0)


def choose(picks, counts, offsets, blocks, keep):
    def add(block, found):
        good = (block < counts[0]) & keep(offsets[block, 0])

        @pl.when(good)
        def _():
            picks[found] = block

        return found + good.astype(jnp.int32)

    return lax.fori_loop(0, blocks, add, 0)


def first_body(offsets, counts, observed, ku_t, kv_t, kv, model, halo, out, picks, obs, grid, acc):
    rows = model.shape[1]
    obs[...] = observed[...].astype(F32)
    grid[:, :rows] = model[...].astype(F32)
    grid[:, rows:] = halo[...].astype(F32)
    acc[...] = jnp.zeros_like(acc)
    limit = choose(picks, counts, offsets, ku_t.shape[0], lambda row: row >= 0)
    grid_blocks(picks, limit, offsets, obs, ku_t, kv_t, kv, grid, acc)
    out[...] = acc[...].astype(BF16)


def border_body(offsets, counts, observed, ku_t, kv_t, kv, model, spill, tail, picks, obs, grid, acc):
    rows = model.shape[1] - SUB
    base = rows - SUB
    obs[...] = observed[...].astype(F32)
    grid[...] = model[...].astype(F32)
    acc[:, base:] = jnp.zeros((4, 2 * SUB, acc.shape[2]), F32)
    limit = choose(picks, counts, offsets, ku_t.shape[0], lambda row: row > base)
    grid_blocks(picks, limit, offsets, obs, ku_t, kv_t, kv, grid, acc)
    spill[...] = acc[:, rows:].astype(BF16)
    tail[...] = acc[:, base:rows]


def inside_body(offsets, counts, observed, ku_t, kv_t, kv, model, tail, out, picks, obs, grid, acc):
    rows = model.shape[1] - SUB
    base = rows - SUB
    obs[...] = observed[...].astype(F32)
    grid[...] = model[...].astype(F32)
    acc[:, :base] = jnp.zeros((4, base, acc.shape[2]), F32)
    acc[:, base:rows] = tail[...]
    limit = choose(picks, counts, offsets, ku_t.shape[0], lambda row: row <= base)
    grid_blocks(picks, limit, offsets, obs, ku_t, kv_t, kv, grid, acc)
    views = out.shape[0]
    quarter = rows // views
    for view in range(views):
        out[view] = acc[:, view * quarter : (view + 1) * quarter].astype(BF16)


def flip(value):
    return value[..., ::-1, ::-1].astype(F32)


def on_device(model, observed, kernels, offsets, counts):
    views = lax.axis_size("vis")
    view = lax.axis_index("vis")
    tiles = lax.axis_size("tile")
    rows, cols = model.shape[1:]
    full = rows + SUB
    quarter = rows // views
    blocks, depth = kernels.shape[:2]
    sds = jax.ShapeDtypeStruct
    scratch = [
        pltpu.SMEM((blocks,), jnp.int32),
        pltpu.VMEM((4, blocks, depth), F32),
        pltpu.VMEM((4, full, cols), F32),
        pltpu.VMEM((4, full, cols), F32),
    ]

    halo = send(model[:, :SUB], lambda tile, view: (tile - 1, view))
    ku_t, kv_t, kv = call(
        prepare_body,
        (
            sds((blocks, SUB, depth), BF16),
            sds((blocks, cols, depth), BF16),
            sds((blocks, depth, cols), BF16),
        ),
        flops=2 * blocks * depth * cols * 320,
        moved=4 * 1024 * 1024,
    )(in_specs=[SMEM, VMEM], out_specs=(VMEM,) * 3)(offsets, kernels)
    flops = 4 * 2 * blocks * depth * cols * SUB * 2
    partial = call(
        first_body, sds((4, full, cols), BF16), scratch, flops=flops, moved=4 * 1024 * 1024
    )(in_specs=[SMEM] * 2 + [VMEM] * 6, out_specs=VMEM)(
        offsets, counts, observed, ku_t, kv_t, kv, model, halo
    )

    parts = lax.all_to_all(partial, "vis", 0, 0, tiled=True)
    own = jnp.sum(parts.astype(F32), axis=0)
    sent = own.astype(BF16)
    across = send(sent[:rows], lambda tile, view: (tiles - 1 - tile, view))
    beside = send(sent[rows - SUB :], lambda tile, view: (tiles - 2 - tile, view))
    before = send(sent[rows:], lambda tile, view: (tile + 1, view))
    after = send(sent[:SUB], lambda tile, view: (tile - 1, view))
    sign = jnp.where(view % 2 == 0, 1.0, -1.0).astype(F32)
    mine = lax.dynamic_index_in_dim(model, view, 0, keepdims=False)
    mine_halo = lax.dynamic_index_in_dim(halo, view, 0, keepdims=False)
    start = jnp.concatenate([mine, mine_halo], axis=0).astype(F32)
    pad = lambda value, low: jnp.pad(value.astype(F32), ((low, full - low - value.shape[0]), (0, 0)))
    summed = own + pad(before, 0) + pad(after, rows)
    mirrored = pad(flip(across), 0) + pad(flip(beside), rows - SUB)
    piece = (start + STEP * (summed + sign * mirrored)).astype(BF16)
    band = lax.all_gather(piece, "vis", axis=0, tiled=False)

    spill, tail = call(
        border_body,
        (sds((4, SUB, cols), BF16), sds((4, SUB, cols), F32)),
        scratch,
        flops=flops // 8,
        moved=4 * 1024 * 1024,
    )(in_specs=[SMEM] * 2 + [VMEM] * 5, out_specs=(VMEM, VMEM))(
        offsets, counts, observed, ku_t, kv_t, kv, band
    )
    spilled = send(spill, lambda tile, view: (tile + 1, view))
    partial = call(
        inside_body,
        sds((views, 4, quarter, cols), BF16),
        scratch,
        flops=flops,
        moved=4 * 1024 * 1024,
    )(in_specs=[SMEM] * 2 + [VMEM] * 6, out_specs=VMEM)(
        offsets, counts, observed, ku_t, kv_t, kv, band, tail
    )
    head = (partial[0, :, :SUB].astype(F32) + spilled.astype(F32)).astype(BF16)
    partial = lax.dynamic_update_slice(partial, head[None], (0, 0, 0, 0))
    parts = lax.all_to_all(partial, "vis", 0, 0, tiled=True)
    own = jnp.sum(parts.astype(F32), axis=0)
    across = send(own.astype(BF16), lambda tile, view: (tiles - 1 - tile, views - 1 - view))
    signs = jnp.array(SIGNS, F32)[:, None, None]
    start = lax.dynamic_slice_in_dim(band, view * quarter, quarter, 1).astype(F32)
    return (start + STEP * (own + signs * flip(across))).astype(BF16)


def solution(mesh):
    placed = (
        P(None, "tile", None),
        P(None, ("tile", "vis"), None),
        P(("tile", "vis"), None, None),
        P(("tile", "vis"), None),
        P(("tile", "vis")),
    )
    return jax.shard_map(
        on_device,
        mesh=mesh,
        in_specs=placed,
        out_specs=P(None, ("tile", "vis"), None),
        check_vma=False,
    )
```

```python
import functools

import jax
import jax.numpy as jnp
from jax import lax
from jax.experimental import pallas as pl
from jax.experimental.pallas import tpu as pltpu
from jax.sharding import PartitionSpec as P

SUB = 64
GROUP = 4
SIGNS = (1.0, -1.0, 1.0, -1.0)
STEP = 0.5 * 0.5
F32 = jnp.float32
BF16 = jnp.bfloat16
VMEM = pl.BlockSpec(memory_space=pltpu.VMEM)
SMEM = pl.BlockSpec(memory_space=pltpu.SMEM)


def send(value, route):
    tiles = lax.axis_size("tile")
    views = lax.axis_size("vis")
    pairs = []
    for tile in range(tiles):
        for view in range(views):
            to_tile, to_view = route(tile, view)
            pairs.append((tile * views + view, to_tile % tiles * views + to_view % views))
    return lax.ppermute(value, ("tile", "vis"), pairs)


def call(body, outs, scratch=(), flops=0, moved=0):
    return functools.partial(
        pl.pallas_call,
        body,
        out_shape=outs,
        scratch_shapes=list(scratch),
        compiler_params=pltpu.CompilerParams(vmem_limit_bytes=40 * 1024 * 1024),
        cost_estimate=pl.CostEstimate(flops=flops, bytes_accessed=moved, transcendentals=0),
    )


def dot_nn(left, right):
    return lax.dot_general(left, right, (((1,), (0,)), ((), ())), preferred_element_type=F32)


def dot_nt(left, right):
    return lax.dot_general(left, right, (((1,), (1,)), ((), ())), preferred_element_type=F32)


def prepare_body(offsets, kern, ku_t, kv_t, kv):
    blocks = kern.shape[0]
    cols = kern.shape[2]

    def one(block):
        shift = SUB - offsets[block, 1]
        row = lax.broadcasted_iota(jnp.int32, (cols, cols), 0)
        col = lax.broadcasted_iota(jnp.int32, (cols, cols), 1)
        place_t = jnp.where((col == row + shift) & (col >= SUB), 1.0, 0.0).astype(BF16)
        place = jnp.where((row == col + shift) & (row >= SUB), 1.0, 0.0).astype(BF16)
        pick = jnp.where(row == col, 1.0, 0.0).astype(BF16)[:SUB]
        weights = kern[block]
        ku_t[block] = dot_nt(pick, weights).astype(BF16)
        kv_t[block] = dot_nt(place_t, weights).astype(BF16)
        kv[block] = dot_nn(weights, place).astype(BF16)

    def group(index, carry):
        for lane in range(GROUP):
            one(index * GROUP + lane)
        return carry

    lax.fori_loop(0, blocks // GROUP, group, 0)


def grid_blocks(picks, limit, offsets, obs, ku_t, kv_t, kv, grid, acc):
    def group(index, carry):
        staged = []
        for lane in range(GROUP):
            place = index * GROUP + lane
            live = place < limit
            block = picks[jnp.minimum(place, limit - 1)]
            row = offsets[block, 0]
            patch = jnp.concatenate(
                [grid[comp, pl.ds(row, SUB), :] for comp in range(4)], axis=0
            ).astype(BF16)
            inner = dot_nn(patch, kv_t[block])
            along_u = ku_t[block].astype(F32)
            parts = []
            for comp in range(4):
                seen = jnp.sum(along_u * inner[comp * SUB : (comp + 1) * SUB], axis=0, keepdims=True)
                left = jnp.where(live, obs[comp, pl.ds(block, 1), :] - seen, 0.0)
                parts.append((along_u * left).astype(BF16))
            fresh = dot_nn(jnp.concatenate(parts, axis=0), kv[block])
            staged.append((row, fresh))
        for row, fresh in staged:
            for comp in range(4):
                acc[comp, pl.ds(row, SUB), :] += fresh[comp * SUB : (comp + 1) * SUB]
        return carry

    lax.fori_loop(0, (limit + GROUP - 1) // GROUP, group, 0)


def choose(picks, counts, offsets, blocks, keep):
    def add(block, found):
        good = (block < counts[0]) & keep(offsets[block, 0])

        @pl.when(good)
        def _():
            picks[found] = block

        return found + good.astype(jnp.int32)

    return lax.fori_loop(0, blocks, add, 0)


def first_body(
    offsets, counts, observed, where, ku_t, kv_t, kv, model, halo, out, picks, obs, grid, acc
):
    rows = model.shape[1]
    full = rows + SUB
    blocks = ku_t.shape[0]
    for half in range(2):
        low = full + half * blocks
        out[:, low : low + blocks] = observed[:, :, half * 128 : (half + 1) * 128]
    for comp in range(4):
        out[comp, full + 2 * blocks :] = where[...]
    obs[...] = observed[...].astype(F32)
    grid[:, :rows] = model[...].astype(F32)
    grid[:, rows:] = halo[...].astype(F32)
    acc[...] = jnp.zeros_like(acc)
    limit = choose(picks, counts, offsets, ku_t.shape[0], lambda row: row >= 0)
    grid_blocks(picks, limit, offsets, obs, ku_t, kv_t, kv, grid, acc)
    out[:, :full] = acc[...].astype(BF16)


def lone_blocks(picks, limit, rows, cols, obs, kern, grid, acc):
    lanes = grid.shape[1]
    high = lax.broadcasted_iota(jnp.int32, (SUB, lanes), 1) >= SUB
    pick = jnp.where(
        lax.broadcasted_iota(jnp.int32, (SUB, lanes), 0)
        == lax.broadcasted_iota(jnp.int32, (SUB, lanes), 1),
        1.0,
        0.0,
    ).astype(BF16)

    def group(index, carry):
        staged = []
        for lane in range(GROUP):
            place = index * GROUP + lane
            live = place < limit
            block = picks[jnp.minimum(place, limit - 1)]
            row = rows[block]
            col = cols[block]
            patch = pltpu.roll(grid[pl.ds(row, SUB), :], SUB - col, 1)
            patch = jnp.where(high, patch, 0.0).astype(BF16)
            weights = kern[block]
            both = dot_nt(jnp.concatenate([pick, patch], axis=0), weights)
            along_u = both[:SUB]
            seen = jnp.sum(along_u * both[SUB:], axis=0, keepdims=True)
            left = jnp.where(live, obs[pl.ds(block, 1), :] - seen, 0.0)
            fresh = dot_nn((along_u * left).astype(BF16), weights)
            fresh = pltpu.roll(jnp.where(high, fresh, 0.0), (SUB + col) % lanes, 1)
            staged.append((row, fresh))
        for row, fresh in staged:
            acc[pl.ds(row, SUB), :] += fresh
        return carry

    lax.fori_loop(0, (limit + GROUP - 1) // GROUP, group, 0)


def choose_rows(picks, rows, keep):
    def add(block, found):
        row = rows[block]
        good = (row >= 0) & keep(row)

        @pl.when(good)
        def _():
            picks[found] = block

        return found + good.astype(jnp.int32)

    return lax.fori_loop(0, rows.shape[0], add, 0)


def spread(observed, obs):
    blocks = observed.shape[1] // 2
    for source in range(observed.shape[0]):
        for half in range(2):
            obs[source * blocks : (source + 1) * blocks, half * 128 : (half + 1) * 128] = observed[
                source, half * blocks : (half + 1) * blocks
            ].astype(F32)


def border_body(rows, cols, observed, kern, model, spill, tail, picks, obs, grid, acc):
    band = model.shape[0] - SUB
    base = band - SUB
    spread(observed, obs)
    grid[...] = model[...].astype(F32)
    acc[base:] = jnp.zeros((2 * SUB, acc.shape[1]), F32)
    limit = choose_rows(picks, rows, lambda row: row > base)
    lone_blocks(picks, limit, rows, cols, obs, kern, grid, acc)
    spill[...] = acc[band:].astype(BF16)
    tail[...] = acc[base:band]


def inside_body(rows, cols, observed, kern, model, tail, out, picks, obs, grid, acc):
    band = model.shape[0] - SUB
    base = band - SUB
    spread(observed, obs)
    grid[...] = model[...].astype(F32)
    acc[:base] = jnp.zeros((base, acc.shape[1]), F32)
    acc[base:band] = tail[...]
    limit = choose_rows(picks, rows, lambda row: row <= base)
    lone_blocks(picks, limit, rows, cols, obs, kern, grid, acc)
    out[...] = acc[:band]


def flip(value):
    return value[..., ::-1, ::-1].astype(F32)


def on_device(model, observed, kernels, offsets, counts):
    views = lax.axis_size("vis")
    view = lax.axis_index("vis")
    tiles = lax.axis_size("tile")
    rows, cols = model.shape[1:]
    full = rows + SUB
    quarter = rows // views
    blocks, depth = kernels.shape[:2]
    sds = jax.ShapeDtypeStruct
    scratch = [
        pltpu.SMEM((blocks,), jnp.int32),
        pltpu.VMEM((4, blocks, depth), F32),
        pltpu.VMEM((4, full, cols), F32),
        pltpu.VMEM((4, full, cols), F32),
    ]

    every = lax.all_gather(kernels, "vis", axis=0, tiled=True)
    live = (jnp.arange(blocks, dtype=jnp.int32) < counts[0]).astype(jnp.int32)
    where = jnp.stack([offsets[:, 0] // 16, offsets[:, 0] % 16, offsets[:, 1], live], axis=1)
    where = jnp.pad(where, ((0, 0), (0, cols - 4))).astype(BF16)
    halo = send(model[:, :SUB], lambda tile, view: (tile - 1, view))
    ku_t, kv_t, kv = call(
        prepare_body,
        (
            sds((blocks, SUB, depth), BF16),
            sds((blocks, cols, depth), BF16),
            sds((blocks, depth, cols), BF16),
        ),
        flops=2 * blocks * depth * cols * 320,
        moved=4 * 1024 * 1024,
    )(in_specs=[SMEM, VMEM], out_specs=(VMEM,) * 3)(offsets, kernels)
    flops = 4 * 2 * blocks * depth * cols * SUB * 2
    partial = call(
        first_body,
        sds((4, full + 3 * blocks, cols), BF16),
        scratch,
        flops=flops,
        moved=4 * 1024 * 1024,
    )(in_specs=[SMEM] * 2 + [VMEM] * 7, out_specs=VMEM)(
        offsets, counts, observed, where, ku_t, kv_t, kv, model, halo
    )

    parts = lax.all_to_all(partial, "vis", 0, 0, tiled=True)
    own = jnp.sum(parts[:, :full].astype(F32), axis=0)
    seen = parts[:, full : full + 2 * blocks]
    where = parts[:, full + 2 * blocks :, :4].astype(jnp.int32).reshape(-1, 4)
    block_rows = jnp.where(where[:, 3] > 0, where[:, 0] * 16 + where[:, 1], -1)
    block_cols = where[:, 2]
    sent = own.astype(BF16)
    across = send(sent[:rows], lambda tile, view: (tiles - 1 - tile, view))
    beside = send(sent[rows - SUB :], lambda tile, view: (tiles - 2 - tile, view))
    before = send(sent[rows:], lambda tile, view: (tile + 1, view))
    after = send(sent[:SUB], lambda tile, view: (tile - 1, view))
    sign = jnp.where(view % 2 == 0, 1.0, -1.0).astype(F32)
    mine = lax.dynamic_index_in_dim(model, view, 0, keepdims=False)
    mine_halo = lax.dynamic_index_in_dim(halo, view, 0, keepdims=False)
    start = jnp.concatenate([mine, mine_halo], axis=0).astype(F32)
    pad = lambda value, low: jnp.pad(value.astype(F32), ((low, full - low - value.shape[0]), (0, 0)))
    summed = own + pad(before, 0) + pad(after, rows)
    mirrored = pad(flip(across), 0) + pad(flip(beside), rows - SUB)
    piece = (start + STEP * (summed + sign * mirrored)).astype(BF16)

    scratch = [
        pltpu.SMEM((views * blocks,), jnp.int32),
        pltpu.VMEM((views * blocks, depth), F32),
        pltpu.VMEM((full, cols), F32),
        pltpu.VMEM((full, cols), F32),
    ]
    spill, tail = call(
        border_body,
        (sds((SUB, cols), BF16), sds((SUB, cols), F32)),
        scratch,
        flops=flops // 8,
        moved=6 * 1024 * 1024,
    )(in_specs=[SMEM] * 2 + [VMEM] * 3, out_specs=(VMEM, VMEM))(
        block_rows, block_cols, seen, every, piece
    )
    spilled = send(spill, lambda tile, view: (tile + 1, view))
    own = call(
        inside_body, sds((rows, cols), F32), scratch, flops=flops, moved=6 * 1024 * 1024
    )(in_specs=[SMEM] * 2 + [VMEM] * 4, out_specs=VMEM)(
        block_rows, block_cols, seen, every, piece, tail
    )
    own = own + jnp.pad(spilled.astype(F32), ((0, rows - SUB), (0, 0)))
    near = (piece[:rows].astype(F32) + STEP * own).astype(BF16).reshape(views, quarter, cols)
    far = own.astype(BF16).reshape(views, quarter, cols)[::-1]

    tile = lax.axis_index("tile")
    low = tile < tiles // 2
    groups = []
    for one in range(tiles // 2):
        groups.append(
            [pick * views + member for pick in (one, tiles - 1 - one) for member in range(views)]
        )
    packed = jnp.where(
        low, jnp.concatenate([near, far], axis=0), jnp.concatenate([far, near], axis=0)
    )
    got = lax.all_to_all(packed, ("tile", "vis"), 0, 0, axis_index_groups=groups, tiled=True)
    signs = jnp.array(SIGNS, F32)[:, None, None]
    near = jnp.where(low, got[:views], got[views:])
    far = jnp.where(low, got[views:], got[:views])
    return (near.astype(F32) + STEP * signs * flip(far)).astype(BF16)


def solution(mesh):
    placed = (
        P(None, "tile", None),
        P(None, ("tile", "vis"), None),
        P(("tile", "vis"), None, None),
        P(("tile", "vis"), None),
        P(("tile", "vis")),
    )
    return jax.shard_map(
        on_device,
        mesh=mesh,
        in_specs=placed,
        out_specs=P(None, ("tile", "vis"), None),
        check_vma=False,
    )
```

```python
import functools

import jax
import jax.numpy as jnp
from jax import lax
from jax.experimental import pallas as pl
from jax.experimental.pallas import tpu as pltpu
from jax.sharding import PartitionSpec as P

SUB = 64
GROUP = 8
WEIGHT = 16
SIGNS = (1.0, -1.0, 1.0, -1.0)
STEP = 0.5 * 0.5
F32 = jnp.float32
BF16 = jnp.bfloat16
VMEM = pl.BlockSpec(memory_space=pltpu.VMEM)
SMEM = pl.BlockSpec(memory_space=pltpu.SMEM)


def send(value, route):
    tiles = lax.axis_size("tile")
    views = lax.axis_size("vis")
    pairs = []
    for tile in range(tiles):
        for view in range(views):
            to_tile, to_view = route(tile, view)
            pairs.append((tile * views + view, to_tile % tiles * views + to_view % views))
    return lax.ppermute(value, ("tile", "vis"), pairs)


def call(body, outs, scratch=(), flops=0, moved=0, vmem=16):
    return functools.partial(
        pl.pallas_call,
        body,
        out_shape=outs,
        scratch_shapes=list(scratch),
        compiler_params=pltpu.CompilerParams(vmem_limit_bytes=vmem * 1024 * 1024),
        cost_estimate=pl.CostEstimate(flops=flops, bytes_accessed=moved, transcendentals=0),
    )


def dot_nn(left, right):
    return lax.dot_general(left, right, (((1,), (0,)), ((), ())), preferred_element_type=F32)


def dot_nt(left, right):
    return lax.dot_general(left, right, (((1,), (1,)), ((), ())), preferred_element_type=F32)


def masks(shift, cols):
    row = lax.broadcasted_iota(jnp.int32, (cols, cols), 0)
    col = lax.broadcasted_iota(jnp.int32, (cols, cols), 1)
    pick = jnp.where(row == col, 1.0, 0.0)[:SUB]
    place_t = jnp.where((col == row + shift) & (col >= SUB), 1.0, 0.0)
    place = jnp.where((row == col + shift) & (row >= SUB), 1.0, 0.0)
    return jnp.concatenate([pick, place_t], axis=0).astype(BF16), place.astype(BF16)


def grid_one(row, live, block, obs, along_u, kv_t, kv, grid):
    patch = jnp.concatenate([grid[comp, pl.ds(row, SUB), :] for comp in range(4)], axis=0)
    inner = dot_nn(patch.astype(BF16), kv_t)
    parts = []
    for comp in range(4):
        seen = jnp.sum(along_u * inner[comp * SUB : (comp + 1) * SUB], axis=0, keepdims=True)
        left = jnp.where(live, obs[comp, pl.ds(block, 1), :] - seen, 0.0)
        parts.append((along_u * left).astype(BF16))
    return dot_nn(jnp.concatenate(parts, axis=0), kv)


def add_one(row, fresh, acc):
    for comp in range(4):
        acc[comp, pl.ds(row, SUB), :] += fresh[comp * SUB : (comp + 1) * SUB]


def prepare_body(offsets, kernels, ku_t, kv_t, kv):
    blocks, _, cols = kernels.shape
    for block in range(blocks):
        both, place = masks(SUB - offsets[1, block], cols)
        weights = kernels[block]
        turned = dot_nt(both, weights).astype(BF16)
        ku_t[block] = turned[:SUB]
        kv_t[block] = turned[SUB:]
        kv[block] = dot_nn(weights, place).astype(BF16)


def grid_all(offsets, counts, base, obs, ku_t, kv_t, kv, grid, acc):
    blocks = ku_t.shape[0]
    for group in range(blocks // GROUP):
        staged = []
        for block in range(group * GROUP, (group + 1) * GROUP):
            row = offsets[0, block]
            live = (block < counts[0]) & (row <= base)
            row = jnp.minimum(row, base)
            along_u = ku_t[block].astype(F32)
            fresh = grid_one(row, live, block, obs, along_u, kv_t[block], kv[block], grid)
            staged.append((row, fresh))
        for row, fresh in staged:
            add_one(row, fresh, acc)


def first_body(offsets, counts, observed, ku_t, kv_t, kv, model, halo, out, obs, grid, acc):
    rows = model.shape[1]
    obs[...] = observed[...].astype(F32)
    grid[:, :rows] = model[...].astype(F32)
    grid[:, rows:] = halo[...].astype(F32)
    acc[...] = jnp.zeros_like(acc)
    grid_all(offsets, counts, rows - 1, obs, ku_t, kv_t, kv, grid, acc)
    out[...] = acc[...].astype(BF16)


def inside_body(offsets, counts, observed, ku_t, kv_t, kv, model, tail, out, obs, grid, acc):
    rows = model.shape[1] - SUB
    base = rows - SUB
    obs[...] = observed[...].astype(F32)
    grid[...] = model[:, :rows].astype(F32)
    acc[:, :base] = jnp.zeros((4, base, acc.shape[2]), F32)
    acc[:, base:] = tail[...]
    grid_all(offsets, counts, base, obs, ku_t, kv_t, kv, grid, acc)
    views = out.shape[0]
    quarter = rows // views
    for view in range(views):
        out[view] = acc[:, view * quarter : (view + 1) * quarter].astype(BF16)


def cross(picks, offsets, counts, obs, ku_t, kv_t, kv, grid, acc, base):
    blocks = ku_t.shape[0]

    def add(block, found):
        good = (block < counts[0]) & (offsets[0, block] > base)

        @pl.when(good)
        def _():
            picks[found] = block

        return found + good.astype(jnp.int32)

    limit = lax.fori_loop(0, blocks, add, 0, unroll=True)

    def pair(index, carry):
        staged = []
        for lane in range(2):
            place = 2 * index + lane
            block = picks[jnp.minimum(place, limit - 1)]
            row = offsets[0, block] - base
            along_u = ku_t[block].astype(F32)
            fresh = grid_one(
                row, place < limit, block, obs, along_u, kv_t[block], kv[block], grid
            )
            staged.append((row, fresh))
        for row, fresh in staged:
            add_one(row, fresh, acc)
        return carry

    lax.fori_loop(0, (limit + 1) // 2, pair, 0)


def border_body(offsets, counts, observed, ku_t, kv_t, kv, model, spill, tail, picks, obs, grid, acc):
    base = model.shape[1] - 2 * SUB
    obs[...] = observed[...].astype(F32)
    grid[...] = model[:, base:].astype(F32)
    acc[...] = jnp.zeros_like(acc)
    cross(picks, offsets, counts, obs, ku_t, kv_t, kv, grid, acc, base)
    spill[...] = acc[:, SUB:].astype(BF16)
    tail[...] = acc[:, :SUB]


def total_body(parts, own, across, beside, before, after):
    rows = across.shape[0]
    total = parts[0].astype(F32)
    for source in range(1, parts.shape[0]):
        total = total + parts[source].astype(F32)
    own[...] = total
    sent = total.astype(BF16)
    across[...] = sent[:rows]
    beside[...] = sent[rows - SUB :]
    before[...] = sent[rows:]
    after[...] = sent[:SUB]


def flip(value):
    return value[..., ::-1, ::-1].astype(F32)


def on_device(model, observed, kernels, offsets, counts):
    views = lax.axis_size("vis")
    view = lax.axis_index("vis")
    tiles = lax.axis_size("tile")
    rows, cols = model.shape[1:]
    full = rows + SUB
    quarter = rows // views
    blocks, depth = kernels.shape[:2]
    sds = jax.ShapeDtypeStruct
    picks = pltpu.SMEM((blocks,), jnp.int32)
    obs = pltpu.VMEM(observed.shape, F32)
    full_rows = pltpu.VMEM((4, full, cols), F32)
    inner_rows = pltpu.VMEM((4, rows, cols), F32)
    end_rows = pltpu.VMEM((4, 2 * SUB, cols), F32)
    flops = 4 * 2 * blocks * depth * cols * SUB * 2
    moved = 4 * 1024 * 1024

    offsets = offsets.T
    halo = send(model[:, :SUB], lambda tile, view: (tile - 1, view))
    ku_t, kv_t, kv = call(
        prepare_body,
        (
            sds((blocks, SUB, depth), BF16),
            sds((blocks, cols, depth), BF16),
            sds((blocks, depth, cols), BF16),
        ),
        flops=WEIGHT * flops,
        moved=moved,
    )(in_specs=[SMEM, VMEM], out_specs=(VMEM,) * 3)(offsets, kernels)
    partial = call(
        first_body,
        sds((4, full, cols), BF16),
        [obs, full_rows, full_rows],
        flops=WEIGHT * flops,
        moved=moved,
    )(in_specs=[SMEM] * 2 + [VMEM] * 6, out_specs=VMEM)(
        offsets, counts, observed, ku_t, kv_t, kv, model, halo
    )

    parts = lax.all_to_all(partial, "vis", 0, 0, tiled=True)
    own, across, beside, before, after = call(
        total_body,
        (
            sds((full, cols), F32),
            sds((rows, cols), BF16),
            sds((2 * SUB, cols), BF16),
            sds((SUB, cols), BF16),
            sds((SUB, cols), BF16),
        ),
        moved=moved,
        vmem=58,
    )(in_specs=[VMEM], out_specs=(VMEM,) * 5)(parts)
    across = send(across, lambda tile, view: (tiles - 1 - tile, view))
    beside = send(beside, lambda tile, view: (tiles - 2 - tile, view))
    before = send(before, lambda tile, view: (tile + 1, view))
    after = send(after, lambda tile, view: (tile - 1, view))
    sign = jnp.where(view % 2 == 0, 1.0, -1.0).astype(F32)
    mine = lax.dynamic_index_in_dim(model, view, 0, keepdims=False)
    mine_halo = lax.dynamic_index_in_dim(halo, view, 0, keepdims=False)
    start = jnp.concatenate([mine, mine_halo], axis=0).astype(F32)
    pad = lambda value, low: jnp.pad(value.astype(F32), ((low, full - low - value.shape[0]), (0, 0)))
    summed = own + pad(before, 0) + pad(after, rows)
    mirrored = pad(flip(across), 0) + pad(flip(beside), rows - SUB)
    piece = (start + STEP * (summed + sign * mirrored)).astype(BF16)
    band = lax.all_gather(piece, "vis", axis=0, tiled=False)

    spill, tail = call(
        border_body,
        (sds((4, SUB, cols), BF16), sds((4, SUB, cols), F32)),
        [picks, obs, end_rows, end_rows],
        flops=flops,
        moved=moved,
    )(in_specs=[SMEM] * 2 + [VMEM] * 5, out_specs=(VMEM, VMEM))(
        offsets, counts, observed, ku_t, kv_t, kv, band
    )
    spilled = send(spill, lambda tile, view: (tile + 1, view))
    partial = call(
        inside_body,
        sds((views, 4, quarter, cols), BF16),
        [obs, inner_rows, inner_rows],
        flops=WEIGHT * flops,
        moved=moved,
    )(in_specs=[SMEM] * 2 + [VMEM] * 6, out_specs=VMEM)(
        offsets, counts, observed, ku_t, kv_t, kv, band, tail
    )
    spilled = jnp.pad(spilled.astype(F32)[None], ((0, views - 1), (0, 0), (0, quarter - SUB), (0, 0)))
    partial = (partial.astype(F32) + spilled).astype(BF16)
    parts = lax.all_to_all(partial, "vis", 0, 0, tiled=True)
    own = jnp.sum(parts.astype(F32), axis=0)
    across = send(own.astype(BF16), lambda tile, view: (tiles - 1 - tile, views - 1 - view))
    signs = jnp.array(SIGNS, F32)[:, None, None]
    start = lax.dynamic_slice_in_dim(band, view * quarter, quarter, 1).astype(F32)
    return (start + STEP * (own + signs * flip(across))).astype(BF16)


def solution(mesh):
    placed = (
        P(None, "tile", None),
        P(None, ("tile", "vis"), None),
        P(("tile", "vis"), None, None),
        P(("tile", "vis"), None),
        P(("tile", "vis")),
    )
    return jax.shard_map(
        on_device,
        mesh=mesh,
        in_specs=placed,
        out_specs=P(None, ("tile", "vis"), None),
        check_vma=False,
    )
```

```python
import functools

import jax
import jax.numpy as jnp
from jax import lax
from jax.experimental import pallas as pl
from jax.experimental.pallas import tpu as pltpu
from jax.sharding import PartitionSpec as P

SUB = 64
GROUP = 8
WEIGHT = 16
SIGNS = (1.0, -1.0, 1.0, -1.0)
STEP = 0.5 * 0.5
F32 = jnp.float32
BF16 = jnp.bfloat16
VMEM = pl.BlockSpec(memory_space=pltpu.VMEM)
SMEM = pl.BlockSpec(memory_space=pltpu.SMEM)


def send(value, route):
    tiles = lax.axis_size("tile")
    views = lax.axis_size("vis")
    pairs = []
    for tile in range(tiles):
        for view in range(views):
            to_tile, to_view = route(tile, view)
            pairs.append((tile * views + view, to_tile % tiles * views + to_view % views))
    return lax.ppermute(value, ("tile", "vis"), pairs)


def call(body, outs, scratch=(), flops=0, moved=0, vmem=16):
    return functools.partial(
        pl.pallas_call,
        body,
        out_shape=outs,
        scratch_shapes=list(scratch),
        compiler_params=pltpu.CompilerParams(vmem_limit_bytes=vmem * 1024 * 1024),
        cost_estimate=pl.CostEstimate(flops=flops, bytes_accessed=moved, transcendentals=0),
    )


def dot_nn(left, right):
    return lax.dot_general(left, right, (((1,), (0,)), ((), ())), preferred_element_type=F32)


def dot_nt(left, right):
    return lax.dot_general(left, right, (((1,), (1,)), ((), ())), preferred_element_type=F32)


def masks(shift, cols):
    row = lax.broadcasted_iota(jnp.int32, (cols, cols), 0)
    col = lax.broadcasted_iota(jnp.int32, (cols, cols), 1)
    pick = jnp.where(row == col, 1.0, 0.0)[:SUB]
    place_t = jnp.where((col == row + shift) & (col >= SUB), 1.0, 0.0)
    place = jnp.where((row == col + shift) & (row >= SUB), 1.0, 0.0)
    return jnp.concatenate([pick, place_t], axis=0).astype(BF16), place.astype(BF16)


def grid_one(row, live, block, obs, along_u, kv_t, kv, grid):
    patch = jnp.concatenate([grid[comp, pl.ds(row, SUB), :] for comp in range(4)], axis=0)
    inner = dot_nn(patch.astype(BF16), kv_t)
    parts = []
    for comp in range(4):
        seen = jnp.sum(along_u * inner[comp * SUB : (comp + 1) * SUB], axis=0, keepdims=True)
        left = jnp.where(live, obs[comp, pl.ds(block, 1), :] - seen, 0.0)
        parts.append((along_u * left).astype(BF16))
    return dot_nn(jnp.concatenate(parts, axis=0), kv)


def add_one(row, fresh, acc):
    for comp in range(4):
        acc[comp, pl.ds(row, SUB), :] += fresh[comp * SUB : (comp + 1) * SUB]


def prepare_body(offsets, kernels, ku_t, kv_t, kv):
    blocks, _, cols = kernels.shape
    for block in range(blocks):
        both, place = masks(SUB - offsets[1, block], cols)
        weights = kernels[block]
        turned = dot_nt(both, weights).astype(BF16)
        ku_t[block] = turned[:SUB]
        kv_t[block] = turned[SUB:]
        kv[block] = dot_nn(weights, place).astype(BF16)


def grid_all(offsets, counts, base, obs, ku_t, kv_t, kv, grid, acc):
    blocks = ku_t.shape[0]
    for group in range(blocks // GROUP):
        staged = []
        for block in range(group * GROUP, (group + 1) * GROUP):
            row = offsets[0, block]
            live = (block < counts[0]) & (row <= base)
            row = jnp.minimum(row, base)
            along_u = ku_t[block].astype(F32)
            fresh = grid_one(row, live, block, obs, along_u, kv_t[block], kv[block], grid)
            staged.append((row, fresh))
        for row, fresh in staged:
            add_one(row, fresh, acc)


def first_body(offsets, counts, observed, ku_t, kv_t, kv, model, halo, out, obs, grid, acc):
    rows = model.shape[1]
    obs[...] = observed[...].astype(F32)
    grid[:, :rows] = model[...].astype(F32)
    grid[:, rows:] = halo[...].astype(F32)
    acc[...] = jnp.zeros_like(acc)
    grid_all(offsets, counts, rows - 1, obs, ku_t, kv_t, kv, grid, acc)
    out[...] = acc[...].astype(BF16)


def inside_body(offsets, counts, observed, ku_t, kv_t, kv, model, tail, out, obs, grid, acc):
    rows = model.shape[1] - SUB
    base = rows - SUB
    obs[...] = observed[...].astype(F32)
    grid[...] = model[:, :rows].astype(F32)
    acc[:, :base] = jnp.zeros((4, base, acc.shape[2]), F32)
    acc[:, base:] = tail[...]
    grid_all(offsets, counts, base, obs, ku_t, kv_t, kv, grid, acc)
    views = out.shape[0]
    quarter = rows // views
    for view in range(views):
        out[view] = acc[:, view * quarter : (view + 1) * quarter].astype(BF16)


def cross(picks, offsets, counts, obs, ku_t, kv_t, kv, grid, acc, base):
    blocks = ku_t.shape[0]

    def add(block, found):
        good = (block < counts[0]) & (offsets[0, block] > base)

        @pl.when(good)
        def _():
            picks[found] = block

        return found + good.astype(jnp.int32)

    limit = lax.fori_loop(0, blocks, add, 0, unroll=True)

    def pair(index, carry):
        staged = []
        for lane in range(2):
            place = 2 * index + lane
            block = picks[jnp.minimum(place, limit - 1)]
            row = offsets[0, block] - base
            along_u = ku_t[block].astype(F32)
            fresh = grid_one(
                row, place < limit, block, obs, along_u, kv_t[block], kv[block], grid
            )
            staged.append((row, fresh))
        for row, fresh in staged:
            add_one(row, fresh, acc)
        return carry

    lax.fori_loop(0, (limit + 1) // 2, pair, 0)


def border_body(offsets, counts, observed, ku_t, kv_t, kv, model, spill, tail, picks, obs, grid, acc):
    base = model.shape[1] - 2 * SUB
    obs[...] = observed[...].astype(F32)
    grid[...] = model[:, base:].astype(F32)
    acc[...] = jnp.zeros_like(acc)
    cross(picks, offsets, counts, obs, ku_t, kv_t, kv, grid, acc, base)
    spill[...] = acc[:, SUB:].astype(BF16)
    tail[...] = acc[:, :SUB]


def total_body(parts, own, across, before, after):
    total = parts[0].astype(F32)
    for source in range(1, parts.shape[0]):
        total = total + parts[source].astype(F32)
    own[...] = total
    sent = total.astype(BF16)
    across[...] = sent[SUB:-SUB]
    before[...] = sent[-2 * SUB :]
    after[...] = sent[:SUB]


def flip(value):
    return value[..., ::-1, ::-1].astype(F32)


def on_device(model, observed, kernels, offsets, counts):
    views = lax.axis_size("vis")
    view = lax.axis_index("vis")
    tiles = lax.axis_size("tile")
    rows, cols = model.shape[1:]
    full = rows + SUB
    quarter = rows // views
    blocks, depth = kernels.shape[:2]
    sds = jax.ShapeDtypeStruct
    picks = pltpu.SMEM((blocks,), jnp.int32)
    obs = pltpu.VMEM(observed.shape, F32)
    full_rows = pltpu.VMEM((4, full, cols), F32)
    inner_rows = pltpu.VMEM((4, rows, cols), F32)
    end_rows = pltpu.VMEM((4, 2 * SUB, cols), F32)
    flops = 4 * 2 * blocks * depth * cols * SUB * 2
    moved = 4 * 1024 * 1024

    offsets = offsets.T
    halo = send(model[:, :SUB], lambda tile, view: (tile - 1, view))
    ku_t, kv_t, kv = call(
        prepare_body,
        (
            sds((blocks, SUB, depth), BF16),
            sds((blocks, cols, depth), BF16),
            sds((blocks, depth, cols), BF16),
        ),
        flops=WEIGHT * flops,
        moved=moved,
    )(in_specs=[SMEM, VMEM], out_specs=(VMEM,) * 3)(offsets, kernels)
    partial = call(
        first_body,
        sds((4, full, cols), BF16),
        [obs, full_rows, full_rows],
        flops=WEIGHT * flops,
        moved=moved,
    )(in_specs=[SMEM] * 2 + [VMEM] * 6, out_specs=VMEM)(
        offsets, counts, observed, ku_t, kv_t, kv, model, halo
    )

    parts = lax.all_to_all(partial, "vis", 0, 0, tiled=True)
    own, across, before, after = call(
        total_body,
        (
            sds((full, cols), F32),
            sds((rows - SUB, cols), BF16),
            sds((2 * SUB, cols), BF16),
            sds((SUB, cols), BF16),
        ),
        moved=moved,
        vmem=58,
    )(in_specs=[VMEM], out_specs=(VMEM,) * 4)(parts)
    across = send(across, lambda tile, view: (tiles - 1 - tile, view))
    before = send(before, lambda tile, view: (tile + 1, view)).astype(F32)
    after = send(after, lambda tile, view: (tile - 1, view))
    beside = (before + jnp.pad(own[:SUB], ((SUB, 0), (0, 0)))).astype(BF16)
    beside = send(beside, lambda tile, view: (tiles - 1 - tile, view))
    sign = jnp.where(view % 2 == 0, 1.0, -1.0).astype(F32)
    mine = lax.dynamic_index_in_dim(model, view, 0, keepdims=False)
    mine_halo = lax.dynamic_index_in_dim(halo, view, 0, keepdims=False)
    start = jnp.concatenate([mine, mine_halo], axis=0).astype(F32)
    pad = lambda value, low: jnp.pad(value.astype(F32), ((low, full - low - value.shape[0]), (0, 0)))
    summed = own + pad(before[SUB:], 0) + pad(after, rows)
    mirrored = pad(flip(across), 0) + pad(flip(beside), rows - SUB)
    piece = (start + STEP * (summed + sign * mirrored)).astype(BF16)
    band = lax.all_gather(piece, "vis", axis=0, tiled=False)

    spill, tail = call(
        border_body,
        (sds((4, SUB, cols), BF16), sds((4, SUB, cols), F32)),
        [picks, obs, end_rows, end_rows],
        flops=flops,
        moved=moved,
    )(in_specs=[SMEM] * 2 + [VMEM] * 5, out_specs=(VMEM, VMEM))(
        offsets, counts, observed, ku_t, kv_t, kv, band
    )
    spilled = send(spill, lambda tile, view: (tile + 1, view))
    partial = call(
        inside_body,
        sds((views, 4, quarter, cols), BF16),
        [obs, inner_rows, inner_rows],
        flops=WEIGHT * flops,
        moved=moved,
    )(in_specs=[SMEM] * 2 + [VMEM] * 6, out_specs=VMEM)(
        offsets, counts, observed, ku_t, kv_t, kv, band, tail
    )
    spilled = jnp.pad(spilled.astype(F32)[None], ((0, views - 1), (0, 0), (0, quarter - SUB), (0, 0)))
    partial = (partial.astype(F32) + spilled).astype(BF16)
    parts = lax.all_to_all(partial, "vis", 0, 0, tiled=True)
    own = jnp.sum(parts.astype(F32), axis=0)
    across = send(own.astype(BF16), lambda tile, view: (tiles - 1 - tile, views - 1 - view))
    signs = jnp.array(SIGNS, F32)[:, None, None]
    start = lax.dynamic_slice_in_dim(band, view * quarter, quarter, 1).astype(F32)
    return (start + STEP * (own + signs * flip(across))).astype(BF16)


def solution(mesh):
    placed = (
        P(None, "tile", None),
        P(None, ("tile", "vis"), None),
        P(("tile", "vis"), None, None),
        P(("tile", "vis"), None),
        P(("tile", "vis")),
    )
    return jax.shard_map(
        on_device,
        mesh=mesh,
        in_specs=placed,
        out_specs=P(None, ("tile", "vis"), None),
        check_vma=False,
    )
```

```python
import functools

import jax
import jax.numpy as jnp
from jax import lax
from jax.experimental import pallas as pl
from jax.experimental.pallas import tpu as pltpu
from jax.sharding import PartitionSpec as P

SUB = 64
GROUP = 8
WEIGHT = 16
SIGNS = (1.0, -1.0, 1.0, -1.0)
STEP = 0.5 * 0.5
F32 = jnp.float32
BF16 = jnp.bfloat16
VMEM = pl.BlockSpec(memory_space=pltpu.VMEM)
SMEM = pl.BlockSpec(memory_space=pltpu.SMEM)


def send(value, route):
    tiles = lax.axis_size("tile")
    views = lax.axis_size("vis")
    pairs = []
    for tile in range(tiles):
        for view in range(views):
            to_tile, to_view = route(tile, view)
            pairs.append((tile * views + view, to_tile % tiles * views + to_view % views))
    return lax.ppermute(value, ("tile", "vis"), pairs)


def with_mirror(value, route):
    tiles = lax.axis_size("tile")
    views = lax.axis_size("vis")
    pairs = []
    for tile in range(tiles // 2):
        for view in range(views):
            to_tile, to_view = route(tile, view)
            pairs.append([tile * views + view, to_tile * views + to_view])
    return lax.all_gather(value, ("tile", "vis"), axis_index_groups=pairs)


def call(body, outs, scratch=(), flops=0, moved=0, vmem=16):
    return functools.partial(
        pl.pallas_call,
        body,
        out_shape=outs,
        scratch_shapes=list(scratch),
        compiler_params=pltpu.CompilerParams(vmem_limit_bytes=vmem * 1024 * 1024),
        cost_estimate=pl.CostEstimate(flops=flops, bytes_accessed=moved, transcendentals=0),
    )


def dot_nn(left, right):
    return lax.dot_general(left, right, (((1,), (0,)), ((), ())), preferred_element_type=F32)


def dot_nt(left, right):
    return lax.dot_general(left, right, (((1,), (1,)), ((), ())), preferred_element_type=F32)


def masks(shift, cols):
    row = lax.broadcasted_iota(jnp.int32, (cols, cols), 0)
    col = lax.broadcasted_iota(jnp.int32, (cols, cols), 1)
    pick = jnp.where(row == col, 1.0, 0.0)[:SUB]
    place_t = jnp.where((col == row + shift) & (col >= SUB), 1.0, 0.0)
    place = jnp.where((row == col + shift) & (row >= SUB), 1.0, 0.0)
    return jnp.concatenate([pick, place_t], axis=0).astype(BF16), place.astype(BF16)


def grid_one(row, live, block, obs, along_u, kv_t, kv, grid):
    patch = jnp.concatenate([grid[comp, pl.ds(row, SUB), :] for comp in range(4)], axis=0)
    inner = dot_nn(patch.astype(BF16), kv_t)
    parts = []
    for comp in range(4):
        seen = jnp.sum(along_u * inner[comp * SUB : (comp + 1) * SUB], axis=0, keepdims=True)
        left = jnp.where(live, obs[comp, pl.ds(block, 1), :] - seen, 0.0)
        parts.append((along_u * left).astype(BF16))
    return dot_nn(jnp.concatenate(parts, axis=0), kv)


def add_one(row, fresh, acc):
    for comp in range(4):
        acc[comp, pl.ds(row, SUB), :] += fresh[comp * SUB : (comp + 1) * SUB]


def prepare_body(offsets, kernels, ku_t, kv_t, kv):
    blocks, _, cols = kernels.shape
    for block in range(blocks):
        both, place = masks(SUB - offsets[1, block], cols)
        weights = kernels[block]
        turned = dot_nt(both, weights).astype(BF16)
        ku_t[block] = turned[:SUB]
        kv_t[block] = turned[SUB:]
        kv[block] = dot_nn(weights, place).astype(BF16)


def grid_all(offsets, counts, base, obs, ku_t, kv_t, kv, grid, acc):
    blocks = ku_t.shape[0]
    for group in range(blocks // GROUP):
        staged = []
        for block in range(group * GROUP, (group + 1) * GROUP):
            row = offsets[0, block]
            live = (block < counts[0]) & (row <= base)
            row = jnp.minimum(row, base)
            along_u = ku_t[block].astype(F32)
            fresh = grid_one(row, live, block, obs, along_u, kv_t[block], kv[block], grid)
            staged.append((row, fresh))
        for row, fresh in staged:
            add_one(row, fresh, acc)


def first_body(offsets, counts, observed, ku_t, kv_t, kv, model, halo, out, obs, grid, acc):
    rows = model.shape[1]
    obs[...] = observed[...].astype(F32)
    grid[:, :rows] = model[...].astype(F32)
    grid[:, rows:] = halo[...].astype(F32)
    acc[...] = jnp.zeros_like(acc)
    grid_all(offsets, counts, rows - 1, obs, ku_t, kv_t, kv, grid, acc)
    out[...] = acc[...].astype(BF16)


def inside_body(offsets, counts, observed, ku_t, kv_t, kv, model, tail, out, obs, grid, acc):
    rows = model.shape[1] - SUB
    base = rows - SUB
    obs[...] = observed[...].astype(F32)
    grid[...] = model[:, :rows].astype(F32)
    acc[:, :base] = jnp.zeros((4, base, acc.shape[2]), F32)
    acc[:, base:] = tail[...]
    grid_all(offsets, counts, base, obs, ku_t, kv_t, kv, grid, acc)
    views = out.shape[0]
    quarter = rows // views
    for view in range(views):
        out[view] = acc[:, view * quarter : (view + 1) * quarter].astype(BF16)


def cross(picks, offsets, counts, obs, ku_t, kv_t, kv, grid, acc, base):
    blocks = ku_t.shape[0]

    def add(block, found):
        good = (block < counts[0]) & (offsets[0, block] > base)

        @pl.when(good)
        def _():
            picks[found] = block

        return found + good.astype(jnp.int32)

    limit = lax.fori_loop(0, blocks, add, 0, unroll=True)

    def pair(index, carry):
        staged = []
        for lane in range(2):
            place = 2 * index + lane
            block = picks[jnp.minimum(place, limit - 1)]
            row = offsets[0, block] - base
            along_u = ku_t[block].astype(F32)
            fresh = grid_one(
                row, place < limit, block, obs, along_u, kv_t[block], kv[block], grid
            )
            staged.append((row, fresh))
        for row, fresh in staged:
            add_one(row, fresh, acc)
        return carry

    lax.fori_loop(0, (limit + 1) // 2, pair, 0)


def border_body(offsets, counts, observed, ku_t, kv_t, kv, model, spill, tail, picks, obs, grid, acc):
    base = model.shape[1] - 2 * SUB
    obs[...] = observed[...].astype(F32)
    grid[...] = model[:, base:].astype(F32)
    acc[...] = jnp.zeros_like(acc)
    cross(picks, offsets, counts, obs, ku_t, kv_t, kv, grid, acc, base)
    spill[...] = acc[:, SUB:].astype(BF16)
    tail[...] = acc[:, :SUB]


def backwards(size):
    row = lax.broadcasted_iota(jnp.int32, (size, size), 0)
    col = lax.broadcasted_iota(jnp.int32, (size, size), 1)
    return jnp.where(row + col == size - 1, 1.0, 0.0).astype(BF16)


def flipped(value):
    turned = dot_nn(value, backwards(value.shape[1])).astype(BF16)
    return dot_nn(backwards(value.shape[0]), turned)


def update_body(place, pair, own, before, after, model, halo, out):
    full = own.shape[0]
    far = place[0]
    view = place[1]
    sign = jnp.where(view % 2 == 0, STEP, -STEP).astype(F32)
    last = full // SUB - 1
    for tile in range(last + 1):
        part = pl.ds(tile * SUB, SUB)
        total = own[part, :]
        if tile == 0:
            total = total + before[SUB:].astype(F32)
        if tile == last:
            total = total + after[...].astype(F32)
            start = halo[view]
        else:
            start = model[view, part, :]
        mirrored = flipped(pair[far, pl.ds((last - tile) * SUB, SUB), :])
        out[part, :] = (start.astype(F32) + STEP * total + sign * mirrored).astype(BF16)


def finish_body(place, pair, own, band, out):
    far = place[0]
    quarter = own.shape[1]
    low = pl.multiple_of(place[1] * quarter, quarter)
    for comp in range(4):
        start = band[comp, pl.ds(low, quarter), :].astype(F32)
        mirrored = flipped(pair[far, comp])
        step = SIGNS[comp] * STEP
        out[comp] = (start + STEP * own[comp] + step * mirrored).astype(BF16)


def on_device(model, observed, kernels, offsets, counts):
    views = lax.axis_size("vis")
    view = lax.axis_index("vis")
    tiles = lax.axis_size("tile")
    tile = lax.axis_index("tile")
    rows, cols = model.shape[1:]
    full = rows + SUB
    quarter = rows // views
    blocks, depth = kernels.shape[:2]
    sds = jax.ShapeDtypeStruct
    picks = pltpu.SMEM((blocks,), jnp.int32)
    obs = pltpu.VMEM(observed.shape, F32)
    full_rows = pltpu.VMEM((4, full, cols), F32)
    inner_rows = pltpu.VMEM((4, rows, cols), F32)
    end_rows = pltpu.VMEM((4, 2 * SUB, cols), F32)
    flops = 4 * 2 * blocks * depth * cols * SUB * 2
    moved = 4 * 1024 * 1024

    offsets = offsets.T
    halo = send(model[:, :SUB], lambda tile, view: (tile - 1, view))
    ku_t, kv_t, kv = call(
        prepare_body,
        (
            sds((blocks, SUB, depth), BF16),
            sds((blocks, cols, depth), BF16),
            sds((blocks, depth, cols), BF16),
        ),
        flops=WEIGHT * flops,
        moved=moved,
    )(in_specs=[SMEM, VMEM], out_specs=(VMEM,) * 3)(offsets, kernels)
    partial = call(
        first_body,
        sds((4, full, cols), BF16),
        [obs, full_rows, full_rows],
        flops=WEIGHT * flops,
        moved=moved,
    )(in_specs=[SMEM] * 2 + [VMEM] * 6, out_specs=VMEM)(
        offsets, counts, observed, ku_t, kv_t, kv, model, halo
    )

    parts = lax.all_to_all(partial, "vis", 0, 0, tiled=True)
    own = jnp.sum(parts.astype(F32), axis=0)
    before = send(own[rows - SUB :].astype(BF16), lambda tile, view: (tile + 1, view))
    after = send(own[:SUB].astype(BF16), lambda tile, view: (tile - 1, view))
    whole = jnp.pad(own[:rows], ((SUB, 0), (0, 0)))
    whole = (whole + jnp.pad(before.astype(F32), ((0, full - 2 * SUB), (0, 0)))).astype(BF16)
    pair = with_mirror(whole, lambda tile, view: (tiles - 1 - tile, view))
    place = jnp.stack([(tile < tiles // 2).astype(jnp.int32), view])
    piece = call(
        update_body,
        sds((full, cols), BF16),
        moved=moved,
    )(in_specs=[SMEM] + [VMEM] * 6, out_specs=VMEM)(
        place, pair, own, before, after, model, halo
    )
    band = lax.all_gather(piece, "vis", axis=0, tiled=False)

    spill, tail = call(
        border_body,
        (sds((4, SUB, cols), BF16), sds((4, SUB, cols), F32)),
        [picks, obs, end_rows, end_rows],
        flops=flops,
        moved=moved,
    )(in_specs=[SMEM] * 2 + [VMEM] * 5, out_specs=(VMEM, VMEM))(
        offsets, counts, observed, ku_t, kv_t, kv, band
    )
    spilled = send(spill, lambda tile, view: (tile + 1, view))
    partial = call(
        inside_body,
        sds((views, 4, quarter, cols), BF16),
        [obs, inner_rows, inner_rows],
        flops=WEIGHT * flops,
        moved=moved,
    )(in_specs=[SMEM] * 2 + [VMEM] * 6, out_specs=VMEM)(
        offsets, counts, observed, ku_t, kv_t, kv, band, tail
    )
    spilled = jnp.pad(spilled.astype(F32)[None], ((0, views - 1), (0, 0), (0, quarter - SUB), (0, 0)))
    partial = (partial.astype(F32) + spilled).astype(BF16)
    parts = lax.all_to_all(partial, "vis", 0, 0, tiled=True)
    own = jnp.sum(parts.astype(F32), axis=0)
    pair = with_mirror(own.astype(BF16), lambda tile, view: (tiles - 1 - tile, views - 1 - view))
    return call(
        finish_body,
        sds((4, quarter, cols), BF16),
        moved=moved,
    )(in_specs=[SMEM] + [VMEM] * 3, out_specs=VMEM)(place, pair, own, band)


def solution(mesh):
    placed = (
        P(None, "tile", None),
        P(None, ("tile", "vis"), None),
        P(("tile", "vis"), None, None),
        P(("tile", "vis"), None),
        P(("tile", "vis")),
    )
    return jax.shard_map(
        on_device,
        mesh=mesh,
        in_specs=placed,
        out_specs=P(None, ("tile", "vis"), None),
        check_vma=False,
    )
```

```python
import functools

import jax
import jax.numpy as jnp
from jax import lax
from jax.experimental import pallas as pl
from jax.experimental.pallas import tpu as pltpu
from jax.sharding import PartitionSpec as P

SUB = 64
GROUP = 8
WEIGHT = 16
SIGNS = (1.0, -1.0, 1.0, -1.0)
STEP = 0.5 * 0.5
F32 = jnp.float32
BF16 = jnp.bfloat16
VMEM = pl.BlockSpec(memory_space=pltpu.VMEM)
SMEM = pl.BlockSpec(memory_space=pltpu.SMEM)


def send(value, route):
    tiles = lax.axis_size("tile")
    views = lax.axis_size("vis")
    pairs = []
    for tile in range(tiles):
        for view in range(views):
            to_tile, to_view = route(tile, view)
            pairs.append((tile * views + view, to_tile % tiles * views + to_view % views))
    return lax.ppermute(value, ("tile", "vis"), pairs)


def with_mirror(value, route):
    tiles = lax.axis_size("tile")
    views = lax.axis_size("vis")
    pairs = []
    for tile in range(tiles // 2):
        for view in range(views):
            to_tile, to_view = route(tile, view)
            pairs.append([tile * views + view, to_tile * views + to_view])
    return lax.all_gather(value, ("tile", "vis"), axis_index_groups=pairs)


def call(body, outs, scratch=(), flops=0, moved=0, vmem=16):
    return functools.partial(
        pl.pallas_call,
        body,
        out_shape=outs,
        scratch_shapes=list(scratch),
        compiler_params=pltpu.CompilerParams(vmem_limit_bytes=vmem * 1024 * 1024),
        cost_estimate=pl.CostEstimate(flops=flops, bytes_accessed=moved, transcendentals=0),
    )


def dot_nn(left, right):
    return lax.dot_general(left, right, (((1,), (0,)), ((), ())), preferred_element_type=F32)


def dot_nt(left, right):
    return lax.dot_general(left, right, (((1,), (1,)), ((), ())), preferred_element_type=F32)


def masks(shift, cols):
    row = lax.broadcasted_iota(jnp.int32, (cols, cols), 0)
    col = lax.broadcasted_iota(jnp.int32, (cols, cols), 1)
    pick = jnp.where(row == col, 1.0, 0.0)[:SUB]
    place_t = jnp.where((col == row + shift) & (col >= SUB), 1.0, 0.0)
    place = jnp.where((row == col + shift) & (row >= SUB), 1.0, 0.0)
    return jnp.concatenate([pick, place_t], axis=0).astype(BF16), place.astype(BF16)


def grid_one(row, live, block, obs, along_u, kv_t, kv, grid):
    patch = jnp.concatenate([grid[comp, pl.ds(row, SUB), :] for comp in range(4)], axis=0)
    inner = dot_nn(patch.astype(BF16), kv_t)
    parts = []
    for comp in range(4):
        seen = jnp.sum(along_u * inner[comp * SUB : (comp + 1) * SUB], axis=0, keepdims=True)
        left = jnp.where(live, obs[comp, pl.ds(block, 1), :] - seen, 0.0)
        parts.append((along_u * left).astype(BF16))
    return dot_nn(jnp.concatenate(parts, axis=0), kv)


def add_one(row, fresh, acc):
    for comp in range(4):
        acc[comp, pl.ds(row, SUB), :] += fresh[comp * SUB : (comp + 1) * SUB]


def prepare_body(table, kernels, ku_t, kv_t, kv):
    blocks, _, cols = kernels.shape
    for block in range(blocks):
        both, place = masks(SUB - table[kernels.shape[0] + block], cols)
        weights = kernels[block]
        turned = dot_nt(both, weights).astype(BF16)
        ku_t[block] = turned[:SUB]
        kv_t[block] = turned[SUB:]
        kv[block] = dot_nn(weights, place).astype(BF16)


def grid_all(table, base, obs, ku_t, kv_t, kv, grid, acc):
    blocks = ku_t.shape[0]
    for group in range(blocks // GROUP):
        staged = []
        for block in range(group * GROUP, (group + 1) * GROUP):
            row = table[block]
            live = (block < table[2 * ku_t.shape[0]]) & (row <= base)
            row = jnp.minimum(row, base)
            along_u = ku_t[block].astype(F32)
            fresh = grid_one(row, live, block, obs, along_u, kv_t[block], kv[block], grid)
            staged.append((row, fresh))
        for row, fresh in staged:
            add_one(row, fresh, acc)


def first_body(table, observed, ku_t, kv_t, kv, model, halo, out, obs, grid, acc):
    rows = model.shape[1]
    obs[...] = observed[...].astype(F32)
    grid[:, :rows] = model[...].astype(F32)
    grid[:, rows:] = halo[...].astype(F32)
    acc[...] = jnp.zeros_like(acc)
    grid_all(table, rows - 1, obs, ku_t, kv_t, kv, grid, acc)
    out[...] = acc[...].astype(BF16)


def inside_body(table, observed, ku_t, kv_t, kv, model, tail, out, obs, grid, acc):
    rows = model.shape[1] - SUB
    base = rows - SUB
    obs[...] = observed[...].astype(F32)
    grid[...] = model[:, :rows].astype(F32)
    acc[:, :base] = jnp.zeros((4, base, acc.shape[2]), F32)
    acc[:, base:] = tail[...]
    grid_all(table, base, obs, ku_t, kv_t, kv, grid, acc)
    views = out.shape[0]
    quarter = rows // views
    for view in range(views):
        out[view] = acc[:, view * quarter : (view + 1) * quarter].astype(BF16)


def cross(picks, table, obs, ku_t, kv_t, kv, grid, acc, base):
    blocks = ku_t.shape[0]

    def add(block, found):
        good = (block < table[2 * ku_t.shape[0]]) & (table[block] > base)

        @pl.when(good)
        def _():
            picks[found] = block

        return found + good.astype(jnp.int32)

    limit = lax.fori_loop(0, blocks, add, 0, unroll=True)

    def pair(index, carry):
        staged = []
        for lane in range(2):
            place = 2 * index + lane
            block = picks[jnp.minimum(place, limit - 1)]
            row = table[block] - base
            along_u = ku_t[block].astype(F32)
            fresh = grid_one(
                row, place < limit, block, obs, along_u, kv_t[block], kv[block], grid
            )
            staged.append((row, fresh))
        for row, fresh in staged:
            add_one(row, fresh, acc)
        return carry

    lax.fori_loop(0, (limit + 1) // 2, pair, 0)


def border_body(table, observed, ku_t, kv_t, kv, model, spill, tail, picks, obs, grid, acc):
    base = model.shape[1] - 2 * SUB
    obs[...] = observed[...].astype(F32)
    grid[...] = model[:, base:].astype(F32)
    acc[...] = jnp.zeros_like(acc)
    cross(picks, table, obs, ku_t, kv_t, kv, grid, acc, base)
    spill[...] = acc[:, SUB:].astype(BF16)
    tail[...] = acc[:, :SUB]


def backwards(size):
    row = lax.broadcasted_iota(jnp.int32, (size, size), 0)
    col = lax.broadcasted_iota(jnp.int32, (size, size), 1)
    return jnp.where(row + col == size - 1, 1.0, 0.0).astype(BF16)


def update_body(table, pair, own, before, after, model, halo, out):
    full = own.shape[0]
    far = table[table.shape[0] - 2]
    view = table[table.shape[0] - 1]
    sign = jnp.where(view % 2 == 0, STEP, -STEP).astype(F32)
    last = full // SUB - 1
    turned = dot_nn(pair[far], backwards(own.shape[1])).astype(BF16)
    swap = backwards(SUB)
    for tile in range(last + 1):
        part = pl.ds(tile * SUB, SUB)
        total = own[part, :]
        if tile == 0:
            total = total + before[SUB:].astype(F32)
        if tile == last:
            total = total + after[...].astype(F32)
            start = halo[view]
        else:
            start = model[view, part, :]
        mirrored = dot_nn(swap, turned[(last - tile) * SUB : (last - tile + 1) * SUB])
        out[part, :] = (start.astype(F32) + STEP * total + sign * mirrored).astype(BF16)


def finish_body(table, pair, own, band, out):
    far = table[table.shape[0] - 2]
    quarter, cols = own.shape[1:]
    low = pl.multiple_of(table[table.shape[0] - 1] * quarter, quarter)
    turned = dot_nn(pair[far].reshape(4 * quarter, cols), backwards(cols)).astype(BF16)
    swap = backwards(quarter)
    for comp in range(4):
        start = band[comp, pl.ds(low, quarter), :].astype(F32)
        mirrored = dot_nn(swap, turned[comp * quarter : (comp + 1) * quarter])
        step = SIGNS[comp] * STEP
        out[comp] = (start + STEP * own[comp] + step * mirrored).astype(BF16)


def on_device(model, observed, kernels, offsets, counts):
    views = lax.axis_size("vis")
    view = lax.axis_index("vis")
    tiles = lax.axis_size("tile")
    tile = lax.axis_index("tile")
    rows, cols = model.shape[1:]
    full = rows + SUB
    quarter = rows // views
    blocks, depth = kernels.shape[:2]
    sds = jax.ShapeDtypeStruct
    picks = pltpu.SMEM((blocks,), jnp.int32)
    obs = pltpu.VMEM(observed.shape, F32)
    full_rows = pltpu.VMEM((4, full, cols), F32)
    inner_rows = pltpu.VMEM((4, rows, cols), F32)
    end_rows = pltpu.VMEM((4, 2 * SUB, cols), F32)
    flops = 4 * 2 * blocks * depth * cols * SUB * 2
    moved = 4 * 1024 * 1024

    low = tile < tiles // 2
    table = jnp.concatenate(
        [offsets[:, 0], offsets[:, 1], counts, jnp.stack([low.astype(jnp.int32), view])]
    )
    halo = send(model[:, :SUB], lambda tile, view: (tile - 1, view))
    ku_t, kv_t, kv = call(
        prepare_body,
        (
            sds((blocks, SUB, depth), BF16),
            sds((blocks, cols, depth), BF16),
            sds((blocks, depth, cols), BF16),
        ),
        flops=WEIGHT * flops,
        moved=moved,
    )(in_specs=[SMEM, VMEM], out_specs=(VMEM,) * 3)(table, kernels)
    partial = call(
        first_body,
        sds((4, full, cols), BF16),
        [obs, full_rows, full_rows],
        flops=WEIGHT * flops,
        moved=moved,
    )(in_specs=[SMEM] + [VMEM] * 6, out_specs=VMEM)(
        table, observed, ku_t, kv_t, kv, model, halo
    )

    partial, table = lax.optimization_barrier((partial, table))
    parts = lax.all_to_all(partial, "vis", 0, 0, tiled=True)
    own = jnp.sum(parts.astype(F32), axis=0)
    before = send(own[rows - SUB :].astype(BF16), lambda tile, view: (tile + 1, view))
    after = send(own[:SUB].astype(BF16), lambda tile, view: (tile - 1, view))
    whole = jnp.pad(own[:rows], ((SUB, 0), (0, 0)))
    whole = (whole + jnp.pad(before.astype(F32), ((0, full - 2 * SUB), (0, 0)))).astype(BF16)
    pair = with_mirror(whole, lambda tile, view: (tiles - 1 - tile, view))
    piece = call(
        update_body,
        sds((full, cols), BF16),
        moved=moved,
    )(in_specs=[SMEM] + [VMEM] * 6, out_specs=VMEM)(
        table, pair, own, before, after, model, halo
    )
    band = lax.all_gather(piece, "vis", axis=0, tiled=False)

    spill, tail = call(
        border_body,
        (sds((4, SUB, cols), BF16), sds((4, SUB, cols), F32)),
        [picks, obs, end_rows, end_rows],
        flops=flops,
        moved=moved,
    )(in_specs=[SMEM] + [VMEM] * 5, out_specs=(VMEM, VMEM))(
        table, observed, ku_t, kv_t, kv, band
    )
    spilled = send(spill, lambda tile, view: (tile + 1, view))
    partial = call(
        inside_body,
        sds((views, 4, quarter, cols), BF16),
        [obs, inner_rows, inner_rows],
        flops=WEIGHT * flops,
        moved=moved,
    )(in_specs=[SMEM] + [VMEM] * 6, out_specs=VMEM)(
        table, observed, ku_t, kv_t, kv, band, tail
    )
    spilled = jnp.pad(spilled.astype(F32)[None], ((0, views - 1), (0, 0), (0, quarter - SUB), (0, 0)))
    partial = (partial.astype(F32) + spilled).astype(BF16)
    parts = lax.all_to_all(partial, "vis", 0, 0, tiled=True)
    own = jnp.sum(parts.astype(F32), axis=0)
    pair = with_mirror(own.astype(BF16), lambda tile, view: (tiles - 1 - tile, views - 1 - view))
    return call(
        finish_body,
        sds((4, quarter, cols), BF16),
        moved=moved,
    )(in_specs=[SMEM] + [VMEM] * 3, out_specs=VMEM)(table, pair, own, band)


def solution(mesh):
    placed = (
        P(None, "tile", None),
        P(None, ("tile", "vis"), None),
        P(("tile", "vis"), None, None),
        P(("tile", "vis"), None),
        P(("tile", "vis")),
    )
    return jax.shard_map(
        on_device,
        mesh=mesh,
        in_specs=placed,
        out_specs=P(None, ("tile", "vis"), None),
        check_vma=False,
    )
```

```python
import functools

import jax
import jax.numpy as jnp
from jax import lax
from jax.experimental import pallas as pl
from jax.experimental.pallas import tpu as pltpu
from jax.sharding import PartitionSpec as P

SUB = 64
GROUP = 8
WEIGHT = 16
SIGNS = (1.0, -1.0, 1.0, -1.0)
STEP = 0.5 * 0.5
F32 = jnp.float32
BF16 = jnp.bfloat16
VMEM = pl.BlockSpec(memory_space=pltpu.VMEM)
SMEM = pl.BlockSpec(memory_space=pltpu.SMEM)


def send(value, route):
    tiles = lax.axis_size("tile")
    views = lax.axis_size("vis")
    pairs = []
    for tile in range(tiles):
        for view in range(views):
            to_tile, to_view = route(tile, view)
            pairs.append((tile * views + view, to_tile % tiles * views + to_view % views))
    return lax.ppermute(value, ("tile", "vis"), pairs)


def with_mirror(value, route):
    tiles = lax.axis_size("tile")
    views = lax.axis_size("vis")
    pairs = []
    for tile in range(tiles // 2):
        for view in range(views):
            to_tile, to_view = route(tile, view)
            pairs.append([tile * views + view, to_tile * views + to_view])
    return lax.all_gather(value, ("tile", "vis"), axis_index_groups=pairs)


def call(body, outs, scratch=(), flops=0, moved=0, vmem=16):
    return functools.partial(
        pl.pallas_call,
        body,
        out_shape=outs,
        scratch_shapes=list(scratch),
        compiler_params=pltpu.CompilerParams(vmem_limit_bytes=vmem * 1024 * 1024),
        cost_estimate=pl.CostEstimate(flops=flops, bytes_accessed=moved, transcendentals=0),
    )


def dot_nn(left, right):
    return lax.dot_general(left, right, (((1,), (0,)), ((), ())), preferred_element_type=F32)


def dot_nt(left, right):
    return lax.dot_general(left, right, (((1,), (1,)), ((), ())), preferred_element_type=F32)


def masks(shift, cols):
    row = lax.broadcasted_iota(jnp.int32, (cols, cols), 0)
    col = lax.broadcasted_iota(jnp.int32, (cols, cols), 1)
    pick = jnp.where(row == col, 1.0, 0.0)[:SUB]
    place = jnp.where((col == row + shift) & (col >= SUB), 1.0, 0.0)
    return jnp.concatenate([pick, place], axis=0).astype(BF16)


def grid_one(row, live, block, obs, along_u, kv_t, grid):
    patch = jnp.concatenate([grid[comp, pl.ds(row, SUB), :] for comp in range(4)], axis=0)
    inner = dot_nn(patch.astype(BF16), kv_t)
    parts = []
    for comp in range(4):
        seen = jnp.sum(along_u * inner[comp * SUB : (comp + 1) * SUB], axis=0, keepdims=True)
        left = jnp.where(live, obs[comp, pl.ds(block, 1), :] - seen, 0.0)
        parts.append((along_u * left).astype(BF16))
    return dot_nt(jnp.concatenate(parts, axis=0), kv_t)


def add_one(row, fresh, acc):
    for comp in range(4):
        acc[comp, pl.ds(row, SUB), :] += fresh[comp * SUB : (comp + 1) * SUB]


def prepare_body(table, kernels, ku_t, kv_t):
    blocks, _, cols = kernels.shape
    for block in range(blocks):
        turned = dot_nt(masks(SUB - table[1, block], cols), kernels[block]).astype(BF16)
        ku_t[block] = turned[:SUB]
        kv_t[block] = turned[SUB:]


def grid_all(table, base, obs, ku_t, kv_t, grid, acc):
    blocks = ku_t.shape[0]
    for group in range(blocks // GROUP):
        staged = []
        for block in range(group * GROUP, (group + 1) * GROUP):
            row = table[0, block]
            live = (block < table[2, 0]) & (row <= base)
            row = jnp.minimum(row, base)
            along_u = ku_t[block].astype(F32)
            fresh = grid_one(row, live, block, obs, along_u, kv_t[block], grid)
            staged.append((row, fresh))
        for row, fresh in staged:
            add_one(row, fresh, acc)


def first_body(table, observed, ku_t, kv_t, model, halo, out, obs, grid, acc):
    rows = model.shape[1]
    obs[...] = observed[...].astype(F32)
    grid[:, :rows] = model[...].astype(F32)
    grid[:, rows:] = halo[...].astype(F32)
    acc[...] = jnp.zeros_like(acc)
    grid_all(table, rows - 1, obs, ku_t, kv_t, grid, acc)
    out[...] = acc[...].astype(BF16)


def inside_body(table, observed, ku_t, kv_t, model, tail, out, obs, grid, acc):
    rows = model.shape[1] - SUB
    base = rows - SUB
    obs[...] = observed[...].astype(F32)
    grid[...] = model[:, :rows].astype(F32)
    acc[:, :base] = jnp.zeros((4, base, acc.shape[2]), F32)
    acc[:, base:] = tail[...]
    grid_all(table, base, obs, ku_t, kv_t, grid, acc)
    views = out.shape[0]
    quarter = rows // views
    for view in range(views):
        out[view] = acc[:, view * quarter : (view + 1) * quarter].astype(BF16)


def cross(picks, table, obs, ku_t, kv_t, grid, acc, base):
    blocks = ku_t.shape[0]

    def add(block, found):
        good = (block < table[2, 0]) & (table[0, block] > base)

        @pl.when(good)
        def _():
            picks[found] = block

        return found + good.astype(jnp.int32)

    limit = lax.fori_loop(0, blocks, add, 0, unroll=True)

    def pair(index, carry):
        staged = []
        for lane in range(2):
            place = 2 * index + lane
            block = picks[jnp.minimum(place, limit - 1)]
            row = table[0, block] - base
            along_u = ku_t[block].astype(F32)
            fresh = grid_one(
                row, place < limit, block, obs, along_u, kv_t[block], grid
            )
            staged.append((row, fresh))
        for row, fresh in staged:
            add_one(row, fresh, acc)
        return carry

    lax.fori_loop(0, (limit + 1) // 2, pair, 0)


def border_body(table, observed, ku_t, kv_t, model, spill, tail, picks, obs, grid, acc):
    base = model.shape[1] - 2 * SUB
    obs[...] = observed[...].astype(F32)
    grid[...] = model[:, base:].astype(F32)
    acc[...] = jnp.zeros_like(acc)
    cross(picks, table, obs, ku_t, kv_t, grid, acc, base)
    spill[...] = acc[:, SUB:].astype(BF16)
    tail[...] = acc[:, :SUB]


def backwards(size):
    row = lax.broadcasted_iota(jnp.int32, (size, size), 0)
    col = lax.broadcasted_iota(jnp.int32, (size, size), 1)
    return jnp.where(row + col == size - 1, 1.0, 0.0).astype(BF16)


def update_body(table, pair, own, before, after, model, halo, out):
    full = own.shape[0]
    far = table[2, 1]
    view = table[2, 2]
    sign = jnp.where(view % 2 == 0, STEP, -STEP).astype(F32)
    last = full // SUB - 1
    turned = dot_nn(pair[far], backwards(own.shape[1])).astype(BF16)
    swap = backwards(SUB)
    for tile in range(last + 1):
        part = pl.ds(tile * SUB, SUB)
        total = own[part, :]
        if tile == 0:
            total = total + before[SUB:].astype(F32)
        if tile == last:
            total = total + after[...].astype(F32)
            start = halo[view]
        else:
            start = model[view, part, :]
        mirrored = dot_nn(swap, turned[(last - tile) * SUB : (last - tile + 1) * SUB])
        out[part, :] = (start.astype(F32) + STEP * total + sign * mirrored).astype(BF16)


def finish_body(table, pair, own, band, out, done, sems):
    far = table[2, 1]
    quarter, cols = own.shape[1:]
    low = pl.multiple_of(table[2, 2] * quarter, quarter)
    turned = dot_nn(pair[far].reshape(4 * quarter, cols), backwards(cols)).astype(BF16)
    swap = backwards(quarter)
    stores = [pltpu.make_async_copy(done.at[comp], out.at[comp], sems.at[comp]) for comp in range(4)]
    for comp in range(4):
        start = band[comp, pl.ds(low, quarter), :].astype(F32)
        mirrored = dot_nn(swap, turned[comp * quarter : (comp + 1) * quarter])
        step = SIGNS[comp] * STEP
        done[comp] = (start + STEP * own[comp] + step * mirrored).astype(BF16)
        stores[comp].start()
    for store in stores:
        store.wait()


def on_device(model, observed, kernels, offsets, counts):
    views = lax.axis_size("vis")
    view = lax.axis_index("vis")
    tiles = lax.axis_size("tile")
    tile = lax.axis_index("tile")
    rows, cols = model.shape[1:]
    full = rows + SUB
    quarter = rows // views
    blocks, depth = kernels.shape[:2]
    sds = jax.ShapeDtypeStruct
    picks = pltpu.SMEM((blocks,), jnp.int32)
    obs = pltpu.VMEM(observed.shape, F32)
    full_rows = pltpu.VMEM((4, full, cols), F32)
    inner_rows = pltpu.VMEM((4, rows, cols), F32)
    end_rows = pltpu.VMEM((4, 2 * SUB, cols), F32)
    flops = 4 * 2 * blocks * depth * cols * SUB * 2
    moved = 4 * 1024 * 1024

    low = tile < tiles // 2
    row = lax.broadcasted_iota(jnp.int32, (3, blocks), 0)
    col = lax.broadcasted_iota(jnp.int32, (3, blocks), 1)
    table = jnp.pad(offsets.T, ((0, 1), (0, 0)))
    for index, item in enumerate((counts[0], low.astype(jnp.int32), view)):
        table = table + jnp.where((row == 2) & (col == index), item, 0)
    halo = send(model[:, :SUB], lambda tile, view: (tile - 1, view))
    ku_t, kv_t = call(
        prepare_body,
        (
            sds((blocks, SUB, depth), BF16),
            sds((blocks, cols, depth), BF16),
        ),
        flops=WEIGHT * flops,
        moved=moved,
    )(in_specs=[SMEM, VMEM], out_specs=(VMEM, VMEM))(table, kernels)
    partial = call(
        first_body,
        sds((4, full, cols), BF16),
        [obs, full_rows, full_rows],
        flops=WEIGHT * flops,
        moved=moved,
    )(in_specs=[SMEM] + [VMEM] * 5, out_specs=VMEM)(
        table, observed, ku_t, kv_t, model, halo
    )

    partial, table = lax.optimization_barrier((partial, table))
    parts = lax.all_to_all(partial, "vis", 0, 0, tiled=True)
    own = jnp.sum(parts.astype(F32), axis=0)
    before = send(own[rows - SUB :].astype(BF16), lambda tile, view: (tile + 1, view))
    after = send(own[:SUB].astype(BF16), lambda tile, view: (tile - 1, view))
    whole = jnp.pad(own[:rows], ((SUB, 0), (0, 0)))
    whole = (whole + jnp.pad(before.astype(F32), ((0, full - 2 * SUB), (0, 0)))).astype(BF16)
    pair = with_mirror(whole, lambda tile, view: (tiles - 1 - tile, view))
    piece = call(
        update_body,
        sds((full, cols), BF16),
        moved=moved,
    )(in_specs=[SMEM] + [VMEM] * 6, out_specs=VMEM)(
        table, pair, own, before, after, model, halo
    )
    band = lax.all_gather(piece, "vis", axis=0, tiled=False)

    spill, tail = call(
        border_body,
        (sds((4, SUB, cols), BF16), sds((4, SUB, cols), F32)),
        [picks, obs, end_rows, end_rows],
        flops=flops,
        moved=moved,
    )(in_specs=[SMEM] + [VMEM] * 4, out_specs=(VMEM, VMEM))(
        table, observed, ku_t, kv_t, band
    )
    spilled = send(spill, lambda tile, view: (tile + 1, view))
    partial = call(
        inside_body,
        sds((views, 4, quarter, cols), BF16),
        [obs, inner_rows, inner_rows],
        flops=WEIGHT * flops,
        moved=moved,
    )(in_specs=[SMEM] + [VMEM] * 5, out_specs=VMEM)(
        table, observed, ku_t, kv_t, band, tail
    )
    spilled = jnp.pad(spilled.astype(F32)[None], ((0, views - 1), (0, 0), (0, quarter - SUB), (0, 0)))
    partial = (partial.astype(F32) + spilled).astype(BF16)
    parts = lax.all_to_all(partial, "vis", 0, 0, tiled=True)
    own = jnp.sum(parts.astype(F32), axis=0)
    pair = with_mirror(own.astype(BF16), lambda tile, view: (tiles - 1 - tile, views - 1 - view))
    return call(
        finish_body,
        sds((4, quarter, cols), BF16),
        [pltpu.VMEM((4, quarter, cols), BF16), pltpu.SemaphoreType.DMA((4,))],
        moved=moved,
    )(in_specs=[SMEM] + [VMEM] * 3, out_specs=pl.BlockSpec(memory_space=pltpu.HBM))(table, pair, own, band)


def solution(mesh):
    placed = (
        P(None, "tile", None),
        P(None, ("tile", "vis"), None),
        P(("tile", "vis"), None, None),
        P(("tile", "vis"), None),
        P(("tile", "vis")),
    )
    return jax.shard_map(
        on_device,
        mesh=mesh,
        in_specs=placed,
        out_specs=P(None, ("tile", "vis"), None),
        check_vma=False,
    )
```

```python
import functools

import jax
import jax.numpy as jnp
from jax import lax
from jax.experimental import pallas as pl
from jax.experimental.pallas import tpu as pltpu
from jax.sharding import PartitionSpec as P

SUB = 64
GROUP = 8
WEIGHT = 16
SIGNS = (1.0, -1.0, 1.0, -1.0)
STEP = 0.5 * 0.5
F32 = jnp.float32
BF16 = jnp.bfloat16
VMEM = pl.BlockSpec(memory_space=pltpu.VMEM)
SMEM = pl.BlockSpec(memory_space=pltpu.SMEM)


def send(value, route):
    tiles = lax.axis_size("tile")
    views = lax.axis_size("vis")
    pairs = []
    for tile in range(tiles):
        for view in range(views):
            to_tile, to_view = route(tile, view)
            pairs.append((tile * views + view, to_tile % tiles * views + to_view % views))
    return lax.ppermute(value, ("tile", "vis"), pairs)


def with_mirror(value, route):
    tiles = lax.axis_size("tile")
    views = lax.axis_size("vis")
    pairs = []
    for tile in range(tiles // 2):
        for view in range(views):
            to_tile, to_view = route(tile, view)
            pairs.append([tile * views + view, to_tile * views + to_view])
    return lax.all_gather(value, ("tile", "vis"), axis_index_groups=pairs)


def call(body, outs, scratch=(), flops=0, moved=0, vmem=16):
    return functools.partial(
        pl.pallas_call,
        body,
        out_shape=outs,
        scratch_shapes=list(scratch),
        compiler_params=pltpu.CompilerParams(vmem_limit_bytes=vmem * 1024 * 1024),
        cost_estimate=pl.CostEstimate(flops=flops, bytes_accessed=moved, transcendentals=0),
    )


def dot_nn(left, right):
    return lax.dot_general(left, right, (((1,), (0,)), ((), ())), preferred_element_type=F32)


def dot_nt(left, right):
    return lax.dot_general(left, right, (((1,), (1,)), ((), ())), preferred_element_type=F32)


def masks(shift, cols):
    row = lax.broadcasted_iota(jnp.int32, (cols, cols), 0)
    col = lax.broadcasted_iota(jnp.int32, (cols, cols), 1)
    pick = jnp.where(row == col, 1.0, 0.0)[:SUB]
    place = jnp.where((col == row + shift) & (col >= SUB), 1.0, 0.0)
    return jnp.concatenate([pick, place], axis=0).astype(BF16)


def grid_one(row, live, block, obs, along_u, kv_t, grid):
    patch = jnp.concatenate([grid[comp, pl.ds(row, SUB), :] for comp in range(4)], axis=0)
    inner = dot_nn(patch.astype(BF16), kv_t)
    parts = []
    for comp in range(4):
        seen = jnp.sum(along_u * inner[comp * SUB : (comp + 1) * SUB], axis=0, keepdims=True)
        left = jnp.where(live, obs[comp, pl.ds(block, 1), :] - seen, 0.0)
        parts.append((along_u * left).astype(BF16))
    return dot_nt(jnp.concatenate(parts, axis=0), kv_t)


def add_one(row, fresh, acc):
    for comp in range(4):
        acc[comp, pl.ds(row, SUB), :] += fresh[comp * SUB : (comp + 1) * SUB]


def prepare_body(table, kernels, ku_t, kv_t):
    blocks, _, cols = kernels.shape
    for block in range(blocks):
        turned = dot_nt(masks(SUB - table[1, block], cols), kernels[block]).astype(BF16)
        ku_t[block] = turned[:SUB]
        kv_t[block] = turned[SUB:]


def grid_all(table, base, obs, ku_t, kv_t, grid, acc):
    blocks = ku_t.shape[0]
    for group in range(blocks // GROUP):
        staged = []
        for block in range(group * GROUP, (group + 1) * GROUP):
            row = table[0, block]
            live = (block < table[2, 0]) & (row <= base)
            row = jnp.minimum(row, base)
            along_u = ku_t[block].astype(F32)
            fresh = grid_one(row, live, block, obs, along_u, kv_t[block], grid)
            staged.append((row, fresh))
        for row, fresh in staged:
            add_one(row, fresh, acc)


def first_body(table, observed, ku_t, kv_t, model, halo, out, obs, grid, acc):
    rows = model.shape[1]
    obs[...] = observed[...].astype(F32)
    grid[:, :rows] = model[...].astype(F32)
    grid[:, rows:] = halo[...].astype(F32)
    acc[...] = jnp.zeros_like(acc)
    grid_all(table, rows - 1, obs, ku_t, kv_t, grid, acc)
    out[...] = acc[...].astype(BF16)


def inside_body(table, observed, ku_t, kv_t, model, tail, out, obs, grid, acc):
    rows = model.shape[1] - SUB
    base = rows - SUB
    obs[...] = observed[...].astype(F32)
    grid[...] = model[:, :rows].astype(F32)
    acc[:, :base] = jnp.zeros((4, base, acc.shape[2]), F32)
    acc[:, base:] = tail[...]
    grid_all(table, base, obs, ku_t, kv_t, grid, acc)
    views = out.shape[0]
    quarter = rows // views
    for view in range(views):
        out[view] = acc[:, view * quarter : (view + 1) * quarter].astype(BF16)


def cross(picks, table, obs, ku_t, kv_t, grid, acc, base):
    blocks = ku_t.shape[0]

    def add(block, found):
        good = (block < table[2, 0]) & (table[0, block] > base)

        @pl.when(good)
        def _():
            picks[found] = block

        return found + good.astype(jnp.int32)

    limit = lax.fori_loop(0, blocks, add, 0, unroll=True)

    def four(index, carry):
        staged = []
        for lane in range(4):
            place = 4 * index + lane
            block = picks[jnp.minimum(place, limit - 1)]
            row = table[0, block] - base
            along_u = ku_t[block].astype(F32)
            fresh = grid_one(
                row, place < limit, block, obs, along_u, kv_t[block], grid
            )
            staged.append((row, fresh))
        for row, fresh in staged:
            add_one(row, fresh, acc)
        return carry

    lax.fori_loop(0, (limit + 3) // 4, four, 0)


def border_body(table, observed, ku_t, kv_t, model, spill, tail, picks, obs, grid, acc):
    base = model.shape[1] - 2 * SUB
    obs[...] = observed[...].astype(F32)
    grid[...] = model[:, base:].astype(F32)
    acc[...] = jnp.zeros_like(acc)
    cross(picks, table, obs, ku_t, kv_t, grid, acc, base)
    spill[...] = acc[:, SUB:].astype(BF16)
    tail[...] = acc[:, :SUB]


def backwards(size):
    row = lax.broadcasted_iota(jnp.int32, (size, size), 0)
    col = lax.broadcasted_iota(jnp.int32, (size, size), 1)
    return jnp.where(row + col == size - 1, 1.0, 0.0).astype(BF16)


def update_body(table, pair, own, before, after, model, halo, out):
    full = own.shape[0]
    far = table[2, 1]
    view = table[2, 2]
    sign = jnp.where(view % 2 == 0, STEP, -STEP).astype(F32)
    last = full // SUB - 1
    turned = dot_nn(pair[far], backwards(own.shape[1])).astype(BF16)
    swap = backwards(SUB)
    for tile in range(last + 1):
        part = pl.ds(tile * SUB, SUB)
        total = own[part, :]
        if tile == 0:
            total = total + before[SUB:].astype(F32)
        if tile == last:
            total = total + after[...].astype(F32)
            start = halo[view]
        else:
            start = model[view, part, :]
        mirrored = dot_nn(swap, turned[(last - tile) * SUB : (last - tile + 1) * SUB])
        out[part, :] = (start.astype(F32) + STEP * total + sign * mirrored).astype(BF16)


def finish_body(table, pair, own, band, out, done, sems):
    far = table[2, 1]
    quarter, cols = own.shape[1:]
    low = pl.multiple_of(table[2, 2] * quarter, quarter)
    turned = dot_nn(pair[far].reshape(4 * quarter, cols), backwards(cols)).astype(BF16)
    swap = backwards(quarter)
    stores = [pltpu.make_async_copy(done.at[comp], out.at[comp], sems.at[comp]) for comp in range(4)]
    for comp in range(4):
        start = band[comp, pl.ds(low, quarter), :].astype(F32)
        mirrored = dot_nn(swap, turned[comp * quarter : (comp + 1) * quarter])
        step = SIGNS[comp] * STEP
        done[comp] = (start + STEP * own[comp] + step * mirrored).astype(BF16)
        stores[comp].start()
    for store in stores:
        store.wait()


def on_device(model, observed, kernels, offsets, counts):
    views = lax.axis_size("vis")
    view = lax.axis_index("vis")
    tiles = lax.axis_size("tile")
    tile = lax.axis_index("tile")
    rows, cols = model.shape[1:]
    full = rows + SUB
    quarter = rows // views
    blocks, depth = kernels.shape[:2]
    sds = jax.ShapeDtypeStruct
    picks = pltpu.SMEM((blocks,), jnp.int32)
    obs = pltpu.VMEM(observed.shape, F32)
    full_rows = pltpu.VMEM((4, full, cols), F32)
    inner_rows = pltpu.VMEM((4, rows, cols), F32)
    end_rows = pltpu.VMEM((4, 2 * SUB, cols), F32)
    flops = 4 * 2 * blocks * depth * cols * SUB * 2
    moved = 4 * 1024 * 1024

    low = tile < tiles // 2
    row = lax.broadcasted_iota(jnp.int32, (3, blocks), 0)
    col = lax.broadcasted_iota(jnp.int32, (3, blocks), 1)
    table = jnp.pad(offsets.T, ((0, 1), (0, 0)))
    for index, item in enumerate((counts[0], low.astype(jnp.int32), view)):
        table = table + jnp.where((row == 2) & (col == index), item, 0)
    halo = send(model[:, :SUB], lambda tile, view: (tile - 1, view))
    ku_t, kv_t = call(
        prepare_body,
        (
            sds((blocks, SUB, depth), BF16),
            sds((blocks, cols, depth), BF16),
        ),
        flops=WEIGHT * flops,
        moved=moved,
    )(in_specs=[SMEM, VMEM], out_specs=(VMEM, VMEM))(table, kernels)
    partial = call(
        first_body,
        sds((4, full, cols), BF16),
        [obs, full_rows, full_rows],
        flops=WEIGHT * flops,
        moved=moved,
    )(in_specs=[SMEM] + [VMEM] * 5, out_specs=VMEM)(
        table, observed, ku_t, kv_t, model, halo
    )

    partial, table = lax.optimization_barrier((partial, table))
    parts = lax.all_to_all(partial, "vis", 0, 0, tiled=True)
    own = jnp.sum(parts.astype(F32), axis=0)
    before = send(own[rows - SUB :].astype(BF16), lambda tile, view: (tile + 1, view))
    after = send(own[:SUB].astype(BF16), lambda tile, view: (tile - 1, view))
    whole = jnp.pad(own[:rows], ((SUB, 0), (0, 0)))
    whole = (whole + jnp.pad(before.astype(F32), ((0, full - 2 * SUB), (0, 0)))).astype(BF16)
    pair = with_mirror(whole, lambda tile, view: (tiles - 1 - tile, view))
    piece = call(
        update_body,
        sds((full, cols), BF16),
        moved=moved,
    )(in_specs=[SMEM] + [VMEM] * 6, out_specs=VMEM)(
        table, pair, own, before, after, model, halo
    )
    band = lax.all_gather(piece, "vis", axis=0, tiled=False)

    spill, tail = call(
        border_body,
        (sds((4, SUB, cols), BF16), sds((4, SUB, cols), F32)),
        [picks, obs, end_rows, end_rows],
        flops=flops,
        moved=moved,
    )(in_specs=[SMEM] + [VMEM] * 4, out_specs=(VMEM, VMEM))(
        table, observed, ku_t, kv_t, band
    )
    spilled = send(spill, lambda tile, view: (tile + 1, view))
    partial = call(
        inside_body,
        sds((views, 4, quarter, cols), BF16),
        [obs, inner_rows, inner_rows],
        flops=WEIGHT * flops,
        moved=moved,
    )(in_specs=[SMEM] + [VMEM] * 5, out_specs=VMEM)(
        table, observed, ku_t, kv_t, band, tail
    )
    spilled = jnp.pad(spilled.astype(F32)[None], ((0, views - 1), (0, 0), (0, quarter - SUB), (0, 0)))
    partial = (partial.astype(F32) + spilled).astype(BF16)
    parts = lax.all_to_all(partial, "vis", 0, 0, tiled=True)
    own = jnp.sum(parts.astype(F32), axis=0)
    pair = with_mirror(own.astype(BF16), lambda tile, view: (tiles - 1 - tile, views - 1 - view))
    return call(
        finish_body,
        sds((4, quarter, cols), BF16),
        [pltpu.VMEM((4, quarter, cols), BF16), pltpu.SemaphoreType.DMA((4,))],
        moved=moved,
    )(in_specs=[SMEM] + [VMEM] * 3, out_specs=pl.BlockSpec(memory_space=pltpu.HBM))(table, pair, own, band)


def solution(mesh):
    placed = (
        P(None, "tile", None),
        P(None, ("tile", "vis"), None),
        P(("tile", "vis"), None, None),
        P(("tile", "vis"), None),
        P(("tile", "vis")),
    )
    return jax.shard_map(
        on_device,
        mesh=mesh,
        in_specs=placed,
        out_specs=P(None, ("tile", "vis"), None),
        check_vma=False,
    )
```

```python
import functools

import jax
import jax.numpy as jnp
from jax import lax
from jax.experimental import pallas as pl
from jax.experimental.pallas import tpu as pltpu
from jax.sharding import PartitionSpec as P

SUB = 64
GROUP = 8
WEIGHT = 16
SIGNS = (1.0, -1.0, 1.0, -1.0)
STEP = 0.5 * 0.5
F32 = jnp.float32
BF16 = jnp.bfloat16
VMEM = pl.BlockSpec(memory_space=pltpu.VMEM)
SMEM = pl.BlockSpec(memory_space=pltpu.SMEM)


def send(value, route):
    tiles = lax.axis_size("tile")
    views = lax.axis_size("vis")
    pairs = []
    for tile in range(tiles):
        for view in range(views):
            to_tile, to_view = route(tile, view)
            pairs.append((tile * views + view, to_tile % tiles * views + to_view % views))
    return lax.ppermute(value, ("tile", "vis"), pairs)


def with_mirror(value, route):
    tiles = lax.axis_size("tile")
    views = lax.axis_size("vis")
    pairs = []
    for tile in range(tiles // 2):
        for view in range(views):
            to_tile, to_view = route(tile, view)
            pairs.append([tile * views + view, to_tile * views + to_view])
    return lax.all_gather(value, ("tile", "vis"), axis_index_groups=pairs)


def call(body, outs, scratch=(), flops=0, moved=0, vmem=16):
    return functools.partial(
        pl.pallas_call,
        body,
        out_shape=outs,
        scratch_shapes=list(scratch),
        compiler_params=pltpu.CompilerParams(vmem_limit_bytes=vmem * 1024 * 1024),
        cost_estimate=pl.CostEstimate(flops=flops, bytes_accessed=moved, transcendentals=0),
    )


def dot_nn(left, right):
    return lax.dot_general(left, right, (((1,), (0,)), ((), ())), preferred_element_type=F32)


def dot_nt(left, right):
    return lax.dot_general(left, right, (((1,), (1,)), ((), ())), preferred_element_type=F32)


def masks(shift, cols):
    row = lax.broadcasted_iota(jnp.int32, (cols, cols), 0)
    col = lax.broadcasted_iota(jnp.int32, (cols, cols), 1)
    pick = jnp.where(row == col, 1.0, 0.0)[:SUB]
    place = jnp.where((col == row + shift) & (col >= SUB), 1.0, 0.0)
    return jnp.concatenate([pick, place], axis=0).astype(BF16)


def grid_one(row, live, block, obs, along_u, kv_t, grid):
    patch = jnp.concatenate([grid[comp, pl.ds(row, SUB), :] for comp in range(4)], axis=0)
    inner = dot_nn(patch.astype(BF16), kv_t)
    parts = []
    for comp in range(4):
        seen = jnp.sum(along_u * inner[comp * SUB : (comp + 1) * SUB], axis=0, keepdims=True)
        left = jnp.where(live, obs[comp, pl.ds(block, 1), :] - seen, 0.0)
        parts.append((along_u * left).astype(BF16))
    return dot_nt(jnp.concatenate(parts, axis=0), kv_t)


def add_one(row, fresh, acc):
    for comp in range(4):
        acc[comp, pl.ds(row, SUB), :] += fresh[comp * SUB : (comp + 1) * SUB]


def prepare_body(table, kernels, ku_t, kv_t):
    blocks, _, cols = kernels.shape
    for block in range(blocks):
        turned = dot_nt(masks(SUB - table[1, block], cols), kernels[block]).astype(BF16)
        ku_t[block] = turned[:SUB]
        kv_t[block] = turned[SUB:]


def grid_all(table, base, obs, ku_t, kv_t, grid, acc):
    blocks = ku_t.shape[0]
    for group in range(blocks // GROUP):
        staged = []
        for block in range(group * GROUP, (group + 1) * GROUP):
            row = table[0, block]
            live = (block < table[2, 0]) & (row <= base)
            row = jnp.minimum(row, base)
            along_u = ku_t[block].astype(F32)
            fresh = grid_one(row, live, block, obs, along_u, kv_t[block], grid)
            staged.append((row, fresh))
        for row, fresh in staged:
            add_one(row, fresh, acc)


def first_body(table, observed, ku_t, kv_t, model, halo, out, obs, grid, acc):
    rows = model.shape[1]
    obs[...] = observed[...].astype(F32)
    grid[:, :rows] = model[...].astype(F32)
    grid[:, rows:] = halo[...].astype(F32)
    acc[...] = jnp.zeros_like(acc)
    grid_all(table, rows - 1, obs, ku_t, kv_t, grid, acc)
    out[...] = acc[...].astype(BF16)


def inside_body(table, observed, ku_t, kv_t, model, tail, out, obs, grid, acc):
    rows = model.shape[1] - SUB
    base = rows - SUB
    obs[...] = observed[...].astype(F32)
    grid[...] = model[:, :rows].astype(F32)
    acc[:, :base] = jnp.zeros((4, base, acc.shape[2]), F32)
    acc[:, base:] = tail[...]
    grid_all(table, base, obs, ku_t, kv_t, grid, acc)
    views = out.shape[0]
    quarter = rows // views
    for view in range(views):
        out[view] = acc[:, view * quarter : (view + 1) * quarter].astype(BF16)


def cross(picks, table, obs, ku_t, kv_t, grid, acc, base):
    blocks = ku_t.shape[0]

    def add(block, found):
        good = (block < table[2, 0]) & (table[0, block] > base)

        @pl.when(good)
        def _():
            picks[found] = block

        return found + good.astype(jnp.int32)

    limit = lax.fori_loop(0, blocks, add, 0, unroll=True)

    def four(index, carry):
        staged = []
        for lane in range(4):
            place = 4 * index + lane
            block = picks[jnp.minimum(place, limit - 1)]
            row = table[0, block] - base
            along_u = ku_t[block].astype(F32)
            fresh = grid_one(
                row, place < limit, block, obs, along_u, kv_t[block], grid
            )
            staged.append((row, fresh))
        for row, fresh in staged:
            add_one(row, fresh, acc)
        return carry

    lax.fori_loop(0, (limit + 3) // 4, four, 0)


def border_body(table, observed, ku_t, kv_t, model, spill, tail, picks, obs, grid, acc):
    base = model.shape[1] - 2 * SUB
    obs[...] = observed[...].astype(F32)
    grid[...] = model[:, base:].astype(F32)
    acc[...] = jnp.zeros_like(acc)
    cross(picks, table, obs, ku_t, kv_t, grid, acc, base)
    spill[...] = acc[:, SUB:].astype(BF16)
    tail[...] = acc[:, :SUB]


def backwards(size):
    row = lax.broadcasted_iota(jnp.int32, (size, size), 0)
    col = lax.broadcasted_iota(jnp.int32, (size, size), 1)
    return jnp.where(row + col == size - 1, 1.0, 0.0).astype(BF16)


def update_body(table, pair, own, before, after, model, halo, out):
    full = own.shape[0]
    far = table[2, 1]
    view = table[2, 2]
    sign = jnp.where(view % 2 == 0, STEP, -STEP).astype(F32)
    last = full // SUB - 1
    turned = dot_nn(pair[far], backwards(own.shape[1])).astype(BF16)
    swap = backwards(SUB)
    for tile in range(last + 1):
        part = pl.ds(tile * SUB, SUB)
        total = own[part, :]
        if tile == 0:
            total = total + before[SUB:].astype(F32)
        if tile == last:
            total = total + after[...].astype(F32)
            start = halo[view]
        else:
            start = model[view, part, :]
        mirrored = dot_nn(swap, turned[(last - tile) * SUB : (last - tile + 1) * SUB])
        out[part, :] = (start.astype(F32) + STEP * total + sign * mirrored).astype(BF16)


def on_device(model, observed, kernels, offsets, counts):
    views = lax.axis_size("vis")
    view = lax.axis_index("vis")
    tiles = lax.axis_size("tile")
    tile = lax.axis_index("tile")
    rows, cols = model.shape[1:]
    full = rows + SUB
    quarter = rows // views
    blocks, depth = kernels.shape[:2]
    sds = jax.ShapeDtypeStruct
    picks = pltpu.SMEM((blocks,), jnp.int32)
    obs = pltpu.VMEM(observed.shape, F32)
    full_rows = pltpu.VMEM((4, full, cols), F32)
    inner_rows = pltpu.VMEM((4, rows, cols), F32)
    end_rows = pltpu.VMEM((4, 2 * SUB, cols), F32)
    flops = 4 * 2 * blocks * depth * cols * SUB * 2
    moved = 4 * 1024 * 1024

    low = tile < tiles // 2
    row = lax.broadcasted_iota(jnp.int32, (3, blocks), 0)
    col = lax.broadcasted_iota(jnp.int32, (3, blocks), 1)
    table = jnp.pad(offsets.T, ((0, 1), (0, 0)))
    for index, item in enumerate((counts[0], low.astype(jnp.int32), view)):
        table = table + jnp.where((row == 2) & (col == index), item, 0)
    halo = send(model[:, :SUB], lambda tile, view: (tile - 1, view))
    ku_t, kv_t = call(
        prepare_body,
        (
            sds((blocks, SUB, depth), BF16),
            sds((blocks, cols, depth), BF16),
        ),
        flops=WEIGHT * flops,
        moved=moved,
    )(in_specs=[SMEM, VMEM], out_specs=(VMEM, VMEM))(table, kernels)
    partial = call(
        first_body,
        sds((4, full, cols), BF16),
        [obs, full_rows, full_rows],
        flops=WEIGHT * flops,
        moved=moved,
    )(in_specs=[SMEM] + [VMEM] * 5, out_specs=VMEM)(
        table, observed, ku_t, kv_t, model, halo
    )

    none = jnp.zeros((), jnp.uint32)
    far_at = low.astype(jnp.uint32)
    first_row = view.astype(jnp.uint32) * quarter
    partial, table, far_at, first_row = lax.optimization_barrier(
        (partial, table, far_at, first_row)
    )
    parts = lax.all_to_all(partial, "vis", 0, 0, tiled=True)
    own = jnp.sum(parts.astype(F32), axis=0)
    before = send(own[rows - SUB :].astype(BF16), lambda tile, view: (tile + 1, view))
    after = send(own[:SUB].astype(BF16), lambda tile, view: (tile - 1, view))
    whole = jnp.pad(own[:rows], ((SUB, 0), (0, 0)))
    whole = (whole + jnp.pad(before.astype(F32), ((0, full - 2 * SUB), (0, 0)))).astype(BF16)
    pair = with_mirror(whole, lambda tile, view: (tiles - 1 - tile, view))
    piece = call(
        update_body,
        sds((full, cols), BF16),
        moved=moved,
    )(in_specs=[SMEM] + [VMEM] * 6, out_specs=VMEM)(
        table, pair, own, before, after, model, halo
    )
    band = lax.all_gather(piece, "vis", axis=0, tiled=False)

    spill, tail = call(
        border_body,
        (sds((4, SUB, cols), BF16), sds((4, SUB, cols), F32)),
        [picks, obs, end_rows, end_rows],
        flops=flops,
        moved=moved,
    )(in_specs=[SMEM] + [VMEM] * 4, out_specs=(VMEM, VMEM))(
        table, observed, ku_t, kv_t, band
    )
    spilled = send(spill, lambda tile, view: (tile + 1, view))
    partial = call(
        inside_body,
        sds((views, 4, quarter, cols), BF16),
        [obs, inner_rows, inner_rows],
        flops=WEIGHT * flops,
        moved=moved,
    )(in_specs=[SMEM] + [VMEM] * 5, out_specs=VMEM)(
        table, observed, ku_t, kv_t, band, tail
    )
    spilled = jnp.pad(spilled.astype(F32)[None], ((0, views - 1), (0, 0), (0, quarter - SUB), (0, 0)))
    partial = (partial.astype(F32) + spilled).astype(BF16)
    parts = lax.all_to_all(partial, "vis", 0, 0, tiled=True)
    own = jnp.sum(parts.astype(F32), axis=0)
    pair = with_mirror(own.astype(BF16), lambda tile, view: (tiles - 1 - tile, views - 1 - view))
    far = lax.dynamic_slice(pair, (far_at, none, none, none), (1, 4, quarter, cols))[0]
    signs = jnp.array(SIGNS, F32)[:, None, None]
    start = lax.dynamic_slice(band, (none, first_row, none), (4, quarter, cols)).astype(F32)
    return (start + STEP * (own + signs * far[:, ::-1, ::-1].astype(F32))).astype(BF16)


def solution(mesh):
    placed = (
        P(None, "tile", None),
        P(None, ("tile", "vis"), None),
        P(("tile", "vis"), None, None),
        P(("tile", "vis"), None),
        P(("tile", "vis")),
    )
    return jax.shard_map(
        on_device,
        mesh=mesh,
        in_specs=placed,
        out_specs=P(None, ("tile", "vis"), None),
        check_vma=False,
    )
```
